512 devices in a mesh: dp: 16 (over z, x_hi), chan: 2 (over core), tm: 16 (over y, x_lo).
Axes of the slice: x: 4 (x_hi: 2, x_lo: 2; x = x_hi * 2 + x_lo), y: 8, z: 8, core: 2. Of those that a mesh axis runs over, the one named last changes fastest.
Arguments:
- inputs: bfloat16 [16, 2, 2048, 1536], P('dp', 'chan', 'tm'), may hold values from -6 to 6
- out_grad: bfloat16 [16, 2, 2048, 1536], P('dp', 'chan', 'tm'), may hold values from -6 to 6
- proj_weight: bfloat16 [1536, 3072], P(('dp', 'chan')), may hold values from -0.15625 to 0.15625
- conv_kernel: float32 [31, 1536], replicated, may hold values from -1 to 1
- norm_mean: float32 [1536], replicated, may hold values from -0.5 to 0.5
- norm_var: float32 [1536], replicated, may hold values from 0.1 to 1
- norm_gain: float32 [1536], replicated, may hold values from 0.1 to 1.9
- norm_bias: float32 [1536], replicated, may hold values from -0.5 to 0.5
- lengths: int32 [16], P('dp'), may hold values from 512 to 2048, as said below
Outputs:
- input_grad: bfloat16 [16, 2, 2048, 1536], P('dp', 'chan', 'tm')
- kernel_grad: float32 [31, 1536], replicated
- gain_grad: float32 [1536], replicated
- bias_grad: float32 [1536], replicated
The draws below stay inside these ranges and needn't reach their ends.
Inputs may be any that keep to these rules, and one draw needn't show every extreme that they name: `lengths`: valid frames of each segment; at least one segment has all 2048.
All inputs are finite; a program needn't handle non-finite values.
Results may differ from the reference program's by a relative error of at most 0.0062.
Values may be sent and summed in bfloat16 or wider, within the bound.
A program may use at most 64 MiB of HBM per device.

```python
import math
import jax
import jax.numpy as jnp
from jax import lax

D = 1536
KERNEL = 31
FRAMES = 2048
SEGMENTS = 16
CHANNELS = 2


def draw_lengths(key, part):
    key = jax.random.fold_in(key, 7)
    first, second = jax.random.split(key)
    drawn = jax.random.randint(first, (SEGMENTS,), FRAMES // 4, FRAMES + 1)
    chosen = jax.random.randint(second, (), 0, SEGMENTS)
    return jnp.where(jnp.arange(SEGMENTS) == chosen, FRAMES, drawn).astype(jnp.int32)


def levels(key, shape, shards, low, largest):
    gain, own = 1.0, jax.random.fold_in(key, 6)
    for axis_at, shards_of in shards:
        draws = jnp.exp(jax.random.uniform(jax.random.fold_in(own, axis_at), (shards_of,), jnp.float32, low / len(shards), largest / len(shards)))
        gain = gain * jnp.repeat(draws, shape[axis_at] // shards_of).reshape([-1 if axis == axis_at else 1 for axis in range(len(shape))])
    return gain


def noise(own_key, shape, width, bound, cuts=(), dtype=jnp.bfloat16):
    factor_of = levels(own_key, shape, cuts, -0.22, 0.18) if cuts else 1.0
    values = jax.random.normal(own_key, shape, jnp.float32) * width * factor_of
    return jnp.minimum(jnp.maximum(values, -bound), bound).astype(dtype)


def setup_inputs(seed: int = 0) -> dict:
    splits = jax.random.split(jax.random.key(seed), 10)
    return {
        "inputs": noise(splits[0], (SEGMENTS, CHANNELS, FRAMES, D), 1.0, 6.0, ((0, 16), (1, 2), (2, 16))),
        "out_grad": noise(splits[1], (SEGMENTS, CHANNELS, FRAMES, D), 1.0, 6.0, ((0, 16), (1, 2), (2, 16))),
        "proj_weight": noise(splits[2], (D, 2 * D), D ** -0.5, 0.15625, ((0, 32),)),
        "conv_kernel": noise(splits[3], (KERNEL, D), KERNEL ** -0.5, 1.0, (), jnp.float32),
        "norm_mean": jnp.clip(jax.random.uniform(splits[4], (D,), jnp.float32, -0.5, 0.5), -0.5, 0.5),
        "norm_var": jnp.clip(jnp.exp(jax.random.uniform(splits[5], (D,), jnp.float32, math.log(0.1), math.log(1.0))), 0.1, 1.0),
        "norm_gain": jnp.clip(1.0 + 0.18 * jax.random.normal(splits[6], (D,), jnp.float32), 0.1, 1.9),
        "norm_bias": jnp.clip(jax.random.uniform(splits[7], (D,), jnp.float32, -0.5, 0.5), -0.5, 0.5),
        "lengths": draw_lengths(jax.random.fold_in(splits[9], 71), 0),
    }


def one_item(item, proj_weight, conv_kernel, norm_mean, norm_var, norm_gain, norm_bias):
    rows, grads, limit = item
    half = KERNEL // 2
    valid = (jnp.arange(FRAMES) < limit).astype(jnp.float32)[:, None]
    pre = jnp.dot(rows, proj_weight, preferred_element_type=jnp.float32)
    value = pre[:, :D]
    gate = jax.nn.sigmoid(pre[:, D:])
    gated = (value * gate * valid).astype(jnp.bfloat16)
    gated_ext = jnp.pad(gated.astype(jnp.float32), ((half, half), (0, 0)))
    conv = jnp.zeros((FRAMES, D), jnp.float32)
    for k in range(KERNEL):
        conv = conv + conv_kernel[k] * gated_ext[k:k + FRAMES]
    rstd = 1.0 / jnp.sqrt(norm_var + 1e-05)
    normed = (conv - norm_mean) * rstd
    act = normed * norm_gain + norm_bias
    sig = jax.nn.sigmoid(act)
    act_grad = grads.astype(jnp.float32) * valid * sig * (1.0 + act * (1.0 - sig))
    conv_grad = (act_grad * norm_gain * rstd).astype(jnp.bfloat16)
    gain_part = lax.optimization_barrier(jnp.sum(act_grad * normed, axis=0))
    bias_part = lax.optimization_barrier(jnp.sum(act_grad, axis=0))
    conv_grad_f = conv_grad.astype(jnp.float32)
    kernel_part = jnp.stack([lax.optimization_barrier(jnp.sum(conv_grad_f * gated_ext[k:k + FRAMES], axis=0)) for k in range(KERNEL)])
    grad_ext = jnp.pad(conv_grad_f, ((half, half), (0, 0)))
    gated_grad = jnp.zeros((FRAMES, D), jnp.float32)
    for k in range(KERNEL):
        gated_grad = gated_grad + conv_kernel[k] * grad_ext[2 * half - k:2 * half - k + FRAMES]
    gated_grad = gated_grad * valid
    pre_grad = jnp.concatenate([gated_grad * gate, gated_grad * value * gate * (1.0 - gate)], axis=1).astype(jnp.bfloat16)
    input_grad = jnp.dot(pre_grad, proj_weight.T, preferred_element_type=jnp.float32).astype(jnp.bfloat16)
    return (input_grad, kernel_part, gain_part, bias_part)

def reference(inputs, out_grad, proj_weight, conv_kernel, norm_mean, norm_var, norm_gain, norm_bias, lengths):
    count = SEGMENTS * CHANNELS
    rows = inputs.reshape(count, FRAMES, D)
    grads = out_grad.reshape(count, FRAMES, D)
    limits = jnp.repeat(lengths, CHANNELS).astype(jnp.int32)

    def step(item):
        return one_item(item, proj_weight, conv_kernel, norm_mean, norm_var, norm_gain, norm_bias)
    input_grad, kernel_parts, gain_parts, bias_parts = lax.map(step, (rows, grads, limits))
    scale = 1.0 / jnp.sqrt(jnp.float32(SEGMENTS * CHANNELS * FRAMES))
    return (input_grad.reshape(SEGMENTS, CHANNELS, FRAMES, D), lax.optimization_barrier(jnp.sum(kernel_parts, axis=0)) * scale, lax.optimization_barrier(jnp.sum(gain_parts, axis=0)) * scale, lax.optimization_barrier(jnp.sum(bias_parts, axis=0)) * scale)
```

```python
import functools

import jax
import jax.numpy as jnp
from jax import lax
from jax.experimental import pallas as pl
from jax.experimental.pallas import tpu as pltpu
from jax.sharding import PartitionSpec as P

MESH = pl.DeviceIdType.MESH
D = 1536
KERNEL = 31
FRAMES = 2048
ROWS = 128
HALO = 32
GHALO = 16
WIDE = ROWS + 2 * HALO
MID = ROWS + 2 * GHALO
SHARD = 48
CW = 128
CHUNKS = D // CW
DP, CHAN, TM = 16, 2, 16
GROUP = TM * CHAN
PART = 24
F32 = jnp.float32
BF16 = jnp.bfloat16
GROUPS = ((0, 6), (6, 12))


def copy_to(src, dst, send, recv, device):
    return pltpu.make_async_remote_copy(
        src_ref=src, dst_ref=dst, send_sem=send, recv_sem=recv, device_id=device, device_id_type=MESH
    )


def await_bytes(ref, sem):
    pltpu.make_async_copy(ref, ref, sem).wait()


def kernel(
    limit, x_in, og_in, w_in, ck, mean, var, gain, bias,
    out, kernel_out, gain_out, bias_out,
    wg, xe, oe, gw, cg, pre, pgr, acc, parts, rb1, rb2, res,
    halo_send, halo_recv, opp_send, opp_recv, z_send, z_recv, y_send, y_recv, s_send, s_recv,
    r1_send, r1_recv, r2_send, r2_recv, r3_send, r3_recv,
):
    dp, c, tm = lax.axis_index("dp"), lax.axis_index("chan"), lax.axis_index("tm")
    z, y = dp // 2, tm // 2
    opp_dp = dp + 1 - 2 * (dp % 2)
    opp_tm = tm + 1 - 2 * (tm % 2)
    me = tm * CHAN + c
    hb = y % 2

    barrier = pltpu.get_barrier_semaphore()

    def greet(i, carry):
        other = lax.rem(me + i, GROUP)
        pl.semaphore_signal(
            barrier, inc=1, device_id=(dp, other % 2, other // 2), device_id_type=MESH
        )
        return carry

    def greet_dp(i, carry):
        pl.semaphore_signal(
            barrier, inc=1, device_id=(lax.rem(dp + i, DP), c, tm), device_id_type=MESH
        )
        return carry

    lax.fori_loop(1, GROUP, greet, 0)
    lax.fori_loop(1, DP, greet_dp, 0)
    pl.semaphore_signal(barrier, inc=1, device_id=(opp_dp, c, opp_tm), device_id_type=MESH)

    for j in range(CHUNKS):
        wg[j, hb, dp, c] = w_in[:, pl.ds(pl.multiple_of(hb * D + j * CW, CW), CW)]
    xe[HALO : HALO + ROWS] = x_in[...]
    oe[GHALO : GHALO + ROWS] = og_in[...]
    pl.semaphore_wait(barrier, GROUP + DP - 1)

    for g, (lo, hi) in enumerate(GROUPS):
        here = wg.at[lo:hi, hb, dp, c]
        copy_to(here, here, opp_send.at[g], opp_recv.at[g], (opp_dp, c, opp_tm)).start()

    right, left = (dp, c, lax.rem(tm + 1, TM)), (dp, c, lax.rem(tm + TM - 1, TM))
    halos = (
        copy_to(x_in.at[ROWS - HALO :], xe.at[0:HALO], halo_send.at[0], halo_recv.at[0], right),
        copy_to(x_in.at[0:HALO], xe.at[HALO + ROWS :], halo_send.at[1], halo_recv.at[1], left),
        copy_to(og_in.at[ROWS - GHALO :], oe.at[0:GHALO], halo_send.at[2], halo_recv.at[2], right),
        copy_to(og_in.at[0:GHALO], oe.at[GHALO + ROWS :], halo_send.at[3], halo_recv.at[3], left),
    )
    for h in halos:
        h.start()

    up = (lax.rem(dp + 2, DP), c, tm)
    down = (lax.rem(dp + DP - 2, DP), c, tm)
    y_even = y + 1 - 2 * (y % 2)
    y_odd = lax.rem(y + 7 + 2 * (y % 2), 8)
    y_partner = tuple((dp, c, p * 2 + tm % 2) for p in (y_even, y_odd))

    def pair(j, zz, h=None):
        return wg.at[j, hb if h is None else h, pl.ds(2 * lax.rem(zz + 8, 8), 2), c]

    def ring_step(j, parity, s):
        ups, downs = (4, 3) if parity == 0 else (3, 4)
        for d, (steps, sign, device) in enumerate(((ups, -1, up), (downs, 1, down))):
            if s > steps:
                continue
            block = pair(j, z + sign * s)
            if s > 0:
                await_bytes(block, z_recv.at[d, j, s - 1])
            if s < steps:
                copy_to(block, block, z_send.at[j], z_recv.at[d, j, s], device).start()
            if s > 0 or d == 0:
                copy_to(block, block, y_send.at[j], y_recv.at[j], y_partner[parity]).start()

    for g, (lo, hi) in enumerate(GROUPS):
        there = wg.at[lo:hi, hb, opp_dp, c]
        await_bytes(there, opp_recv.at[g])
        for s in range(5):

            def both(i, carry):
                for parity in range(2):
                    ring_step(lo + 2 * i + parity, parity, s)
                return carry

            lax.fori_loop(0, (hi - lo) // 2, both, 0)

    def relay(j, carry):
        await_bytes(wg.at[j, 1 - hb, :, c], y_recv.at[j])
        mine = wg.at[j, :, :, c]
        copy_to(mine, mine, s_send.at[j], s_recv.at[j], (dp, 1 - c, tm)).start()
        return carry

    lax.fori_loop(0, CHUNKS, relay, 0)
    for h in halos:
        h.wait()

    t = lax.broadcasted_iota(jnp.int32, (WIDE, CW), 0) + (tm * ROWS - HALO)
    keep = ((t >= 0) & (t < limit[0])).astype(F32)
    keep_mid = keep[HALO - GHALO : HALO + ROWS + GHALO]
    acc[...] = jnp.zeros_like(acc)

    def chunk(j, carry):
        await_bytes(wg.at[j, :, :, 1 - c], s_recv.at[j])
        cs = pl.ds(pl.multiple_of(j * CW, CW), CW)
        w = jnp.concatenate([wg[j, h].reshape(D, CW) for h in range(2)], axis=1)
        pre[...] = jnp.dot(xe[...], w, preferred_element_type=F32)
        sg = lax.logistic(pre[:, CW:])
        gw[...] = (pre[:, :CW] * sg * keep).astype(BF16).astype(F32)
        pre[:, CW:] = sg
        rstd = 1.0 / jnp.sqrt(var[0:1, cs] + 1e-05)
        scale = gain[0:1, cs] * rstd
        gs = jnp.zeros((8, CW), F32)
        bs = jnp.zeros((8, CW), F32)
        step = 80
        for r in range(0, MID, step):
            a = jnp.zeros((step, CW), F32)
            for k in range(KERNEL):
                a = a + ck[k : k + 1, cs] * gw[r + k + 1 : r + k + 1 + step, :]
            normed = (a - mean[0:1, cs]) * rstd
            act = normed * gain[0:1, cs] + bias[0:1, cs]
            sig = lax.logistic(act)
            ag = oe[r : r + step, cs].astype(F32) * keep_mid[r : r + step] * sig
            ag = ag * (1.0 + act * (1.0 - sig))
            cg[r : r + step] = (ag * scale).astype(BF16).astype(F32)
            lo, hi = max(r, GHALO) - r, min(r + step, GHALO + ROWS) - r
            gs = gs + jnp.sum((ag * normed)[lo:hi].reshape((hi - lo) // 8, 8, CW), axis=0)
            bs = bs + jnp.sum(ag[lo:hi].reshape((hi - lo) // 8, 8, CW), axis=0)
        own = cg[GHALO : GHALO + ROWS]
        for k in range(KERNEL):
            s = jnp.sum(own * gw[k + 17 : k + 17 + ROWS], axis=0, keepdims=True)
            parts[j, k // PART, k % PART : k % PART + 1] = s
        parts[j, 1, 7:8] = jnp.sum(gs, axis=0, keepdims=True)
        parts[j, 1, 8:9] = jnp.sum(bs, axis=0, keepdims=True)
        parts[j, 1, 9:] = jnp.zeros((PART - 9, CW), F32)
        step = 64
        for r in range(0, ROWS, step):
            a = jnp.zeros((step, CW), F32)
            for k in range(KERNEL):
                a = a + ck[k : k + 1, cs] * cg[r + 31 - k : r + 31 - k + step]
            a = a * keep_mid[GHALO + r : GHALO + r + step]
            value = pre[HALO + r : HALO + r + step, :CW]
            sg = pre[HALO + r : HALO + r + step, CW:]
            a = a * sg
            pgr[r : r + step, :CW] = a.astype(BF16)
            pgr[r : r + step, CW:] = (a * value * (1.0 - sg)).astype(BF16)
        acc[...] += lax.dot_general(
            pgr[...], w, (((1,), (1,)), ((), ())), preferred_element_type=F32
        )
        for piece in range(2):
            home = (tm == j) & (c == piece)

            @pl.when(home)
            def _():
                rb1[me] = parts[j, piece]

            @pl.when(jnp.logical_not(home))
            def _():
                copy_to(
                    parts.at[j, piece], rb1.at[me], r1_send.at[j, piece], r1_recv, (dp, piece, j)
                ).start()

        return carry

    lax.fori_loop(0, CHUNKS, chunk, 0)
    out[...] = acc[...].astype(BF16)

    @pl.when(tm < CHUNKS)
    def _():
        await_bytes(rb1.at[0 : GROUP - 1], r1_recv)
        total = rb1[0]
        for i in range(1, GROUP):
            total = total + rb1[i]
        rb2[dp] = total

        def spread(i, carry):
            copy_to(
                rb2.at[dp], rb2.at[dp], r2_send.at[i], r2_recv, (lax.rem(dp + i, DP), c, tm)
            ).start()
            return carry

        lax.fori_loop(1, DP, spread, 0)
        await_bytes(rb2.at[0 : DP - 1], r2_recv)
        total = rb2[0]
        for i in range(1, DP):
            total = total + rb2[i]
        res[tm, c] = total * (1.0 / 256.0)

        def share(i, carry):
            other = lax.rem(me + i, GROUP)
            copy_to(
                res.at[tm, c], res.at[tm, c], r3_send.at[i], r3_recv.at[tm, c],
                (dp, other % 2, other // 2),
            ).start()
            return carry

        lax.fori_loop(1, GROUP, share, 0)

    for j in range(CHUNKS):
        for piece in range(2):

            @pl.when(jnp.logical_not((tm == j) & (c == piece)))
            def _():
                await_bytes(res.at[j, piece], r3_recv.at[j, piece])
                await_bytes(parts.at[j, piece], r1_send.at[j, piece])

        cols = slice(j * CW, (j + 1) * CW)
        kernel_out[0:PART, cols] = res[j, 0]
        kernel_out[PART:KERNEL, cols] = res[j, 1, 0 : KERNEL - PART]
        gain_out[:, cols] = res[j, 1, 7:8]
        bias_out[:, cols] = res[j, 1, 8:9]

    for g, (lo, hi) in enumerate(GROUPS):
        await_bytes(wg.at[lo:hi, hb, dp, c], opp_send.at[g])

    def sent(j, carry):
        await_bytes(wg.at[j, 0, 0:14, 0], z_send.at[j])
        await_bytes(wg.at[j, 0, :, 0], y_send.at[j])
        await_bytes(wg.at[j, :, :, c], s_send.at[j])
        return carry

    lax.fori_loop(0, CHUNKS, sent, 0)

    @pl.when(tm < CHUNKS)
    def _():
        def done(i, carry):
            await_bytes(rb2.at[0], r2_send.at[i])
            return carry

        def done3(i, carry):
            await_bytes(res.at[0, 0], r3_send.at[i])
            return carry

        lax.fori_loop(1, DP, done, 0)
        lax.fori_loop(1, GROUP, done3, 0)


def per_device(
    inputs, out_grad, proj_weight, conv_kernel, norm_mean, norm_var, norm_gain, norm_bias, lengths
):
    vmem = pl.BlockSpec(memory_space=pltpu.VMEM)
    dma = pltpu.SemaphoreType.DMA
    row = lambda a: a.reshape(1, D)
    grad, kernel_grad, gain_grad, bias_grad = pl.pallas_call(
        kernel,
        out_shape=(
            jax.ShapeDtypeStruct((ROWS, D), BF16),
            jax.ShapeDtypeStruct((KERNEL, D), F32),
            jax.ShapeDtypeStruct((1, D), F32),
            jax.ShapeDtypeStruct((1, D), F32),
        ),
        in_specs=[pl.BlockSpec(memory_space=pltpu.SMEM)] + [vmem] * 8,
        out_specs=(vmem,) * 4,
        scratch_shapes=[
            pltpu.VMEM((CHUNKS, 2, DP, CHAN, SHARD, CW), BF16),
            pltpu.VMEM((WIDE, D), BF16),
            pltpu.VMEM((MID, D), BF16),
            pltpu.VMEM((WIDE, CW), F32),
            pltpu.VMEM((MID, CW), F32),
            pltpu.VMEM((WIDE, 2 * CW), F32),
            pltpu.VMEM((ROWS, 2 * CW), BF16),
            pltpu.VMEM((ROWS, D), F32),
            pltpu.VMEM((CHUNKS, 2, PART, CW), F32),
            pltpu.VMEM((GROUP, PART, CW), F32),
            pltpu.VMEM((DP, PART, CW), F32),
            pltpu.VMEM((CHUNKS, 2, PART, CW), F32),
            dma((4,)), dma((4,)),
            dma((len(GROUPS),)), dma((len(GROUPS),)),
            dma((CHUNKS,)), dma((2, CHUNKS, 4)),
            dma((CHUNKS,)), dma((CHUNKS,)),
            dma((CHUNKS,)), dma((CHUNKS,)),
            dma((CHUNKS, 2)), dma,
            dma((DP,)), dma,
            dma((GROUP,)), dma((CHUNKS, 2)),
        ],
        compiler_params=pltpu.CompilerParams(
            collective_id=0, has_side_effects=True, vmem_limit_bytes=48 << 20
        ),
    )(
        lengths, inputs.reshape(ROWS, D), out_grad.reshape(ROWS, D), proj_weight, conv_kernel,
        row(norm_mean), row(norm_var), row(norm_gain), row(norm_bias),
    )
    return (
        grad.reshape(1, 1, ROWS, D),
        kernel_grad,
        gain_grad.reshape(D),
        bias_grad.reshape(D),
    )


def solution(mesh):
    in_specs = (
        P("dp", "chan", "tm", None),
        P("dp", "chan", "tm", None),
        P(("dp", "chan"), None),
        P(),
        P(),
        P(),
        P(),
        P(),
        P("dp"),
    )
    out_specs = (P("dp", "chan", "tm", None), P(), P(), P())
    return jax.shard_map(
        per_device, mesh=mesh, in_specs=in_specs, out_specs=out_specs, check_vma=False
    )
```

```python
import functools

import jax
import jax.numpy as jnp
from jax import lax
from jax.experimental import pallas as pl
from jax.experimental.pallas import tpu as pltpu
from jax.sharding import PartitionSpec as P

MESH = pl.DeviceIdType.MESH
D = 1536
KERNEL = 31
FRAMES = 2048
ROWS = 128
SPAN = 2 * ROWS
HALO = 32
GHALO = 16
WIDE = SPAN + 2 * HALO
MID = SPAN + 2 * GHALO
SHARD = 48
CW = 128
HALF = D // 2
CHUNKS = HALF // CW
DP, CHAN, TM = 16, 2, 16
GROUP = TM * CHAN
SUB = GROUP // 2
F32 = jnp.float32
BF16 = jnp.bfloat16
TILES = CHUNKS * 5
LAST = TILES - SUB


def copy_to(src, dst, send, recv, device):
    return pltpu.make_async_remote_copy(
        src_ref=src, dst_ref=dst, send_sem=send, recv_sem=recv, device_id=device, device_id_type=MESH
    )


def await_bytes(ref, sem):
    pltpu.make_async_copy(ref, ref, sem).wait()


def kernel(
    limit, x_in, og_in, w_in, ck_in, mean_in, var_in, gain_in, bias_in,
    out, kernel_out, gain_out, bias_out,
    wg, xe, oe, ck, vecs, rows, pre, gw, cg, near, pgr, acc, away, back, parts, rb1, rb2, res,
    in_sem, w_sem, pair_send, pair_recv, halo_send, halo_recv, opp_send, opp_recv, z_send, z_recv,
    y_send, y_recv, s_send, s_recv, r1_send, r1_recv, r2_send, r2_recv, r3_send, r3_recv,
    out_send, out_recv,
):
    dp, c, tm = lax.axis_index("dp"), lax.axis_index("chan"), lax.axis_index("tm")
    z, xh, y, xl = dp // 2, dp % 2, tm // 2, tm % 2
    opp_dp = dp + 1 - 2 * xh
    opposite = (opp_dp, c, tm + 1 - 2 * xl)
    partner = (dp, c, tm + 1 - 2 * xl)
    me = tm * CHAN + c
    mine = y * CHAN + c
    hb = y % 2

    def weight_cols(half, j):
        return pl.ds(pl.multiple_of(hb * D + half * HALF + j * CW, CW), CW)

    def own_rows(j):
        return pltpu.make_async_copy(
            w_in.at[:, weight_cols(xl, j)], wg.at[j, hb, dp, c], w_sem.at[j]
        )

    def fetch(j, carry):
        own_rows(j).start()
        return carry

    lax.fori_loop(0, CHUNKS, fetch, 0)
    own_at = pl.multiple_of(xl * ROWS, ROWS)
    here = pl.ds(own_at, ROWS)
    x_rows = xe.at[pl.ds(pl.multiple_of(HALO + xl * ROWS, HALO), ROWS)]
    og_rows = oe.at[pl.ds(pl.multiple_of(GHALO + xl * ROWS, GHALO), ROWS)]

    def half_cols(half):
        return pl.ds(pl.multiple_of(half * HALF, HALF), HALF)

    loads = [
        pltpu.make_async_copy(src, dst, in_sem.at[i])
        for i, (src, dst) in enumerate(
            (
                (x_in, x_rows),
                (og_in.at[:, half_cols(xl)], og_rows),
                (ck_in, ck),
                (mean_in, vecs.at[0]),
                (var_in, vecs.at[1]),
                (gain_in, vecs.at[2]),
                (bias_in, vecs.at[3]),
            )
        )
    ]
    for load in loads:
        load.start()

    barrier = pltpu.get_barrier_semaphore()

    def greet(i, carry):
        other = lax.rem(me + i, GROUP)
        pl.semaphore_signal(
            barrier, inc=1, device_id=(dp, other % 2, other // 2), device_id_type=MESH
        )
        return carry

    def greet_dp(i, carry):
        pl.semaphore_signal(
            barrier, inc=1, device_id=(lax.rem(dp + i, DP), c, tm), device_id_type=MESH
        )
        return carry

    pl.semaphore_signal(barrier, inc=1, device_id=opposite, device_id_type=MESH)
    lax.fori_loop(1, DP, greet_dp, 0)
    lax.fori_loop(1, GROUP, greet, 0)
    pl.semaphore_wait(barrier, GROUP + DP - 1)

    def to_opposite(j, carry):
        copy_to(
            w_in.at[:, weight_cols(1 - xl, j)], wg.at[j, hb, dp, c], opp_send, opp_recv, opposite
        ).start()
        return carry

    lax.fori_loop(0, CHUNKS, to_opposite, 0)

    def fetched(j, carry):
        own_rows(j).wait()
        return carry

    lax.fori_loop(0, CHUNKS, fetched, 0)

    up = (lax.rem(dp + 2, DP), c, tm)
    down = (lax.rem(dp + DP - 2, DP), c, tm)
    y_even = y + 1 - 2 * (y % 2)
    y_odd = lax.rem(y + 7 + 2 * (y % 2), 8)

    def ring_step(q, j, s):
        odd = j % 2
        sharer = (dp, c, (y_even * (1 - odd) + y_odd * odd) * 2 + xl)
        part = xh + q - 2 * q * xh
        for d, (steps, sign, device) in enumerate(((4 - odd, 7, up), (3 + odd, 1, down))):
            block = wg.at[j, hb, 2 * lax.rem(z + sign * s, 8) + part, c]

            @pl.when((s > 0) & (s <= steps))
            def _():
                await_bytes(block, z_recv.at[d, q, j, s - 1])

            @pl.when(s < steps)
            def _():
                copy_to(block, block, z_send.at[j], z_recv.at[d, q, j, s], device).start()

            @pl.when((s <= steps) & (s + 1 - d > 0))
            def _():
                copy_to(block, block, y_send.at[j], y_recv.at[j], sharer).start()

    def ring_steps(q, s):
        def one(j, carry):
            ring_step(q, j, s)
            return carry

        lax.fori_loop(0, CHUNKS, one, 0)

    ring_steps(0, 0)

    pair = (
        copy_to(x_in, x_rows, pair_send.at[0], pair_recv.at[0], partner),
        copy_to(
            og_in.at[:, half_cols(1 - xl)], og_rows, pair_send.at[1], pair_recv.at[1], partner
        ),
    )
    for p in pair:
        p.start()
    beyond = lax.rem(y + 7 + 2 * xl, 8) * 2
    x_edge = x_in.at[pl.ds(pl.multiple_of(xl * (ROWS - HALO), HALO), HALO)]
    x_far = xe.at[pl.ds(pl.multiple_of((1 - xl) * (HALO + SPAN), HALO), HALO)]
    og_edge = pl.ds(pl.multiple_of(xl * (ROWS - GHALO), GHALO), GHALO)
    og_far = oe.at[pl.ds(pl.multiple_of((1 - xl) * (GHALO + SPAN), GHALO), GHALO)]
    halos = []
    for other in range(2):
        device = (dp, c, beyond + other)
        halos.append(copy_to(x_edge, x_far, halo_send.at[other], halo_recv.at[xl], device))
        halos.append(
            copy_to(
                og_in.at[og_edge, other * HALF : (other + 1) * HALF], og_far,
                halo_send.at[2 + other], halo_recv.at[2 + xl], device,
            )
        )
    for h in halos:
        h.start()

    await_bytes(wg.at[:, hb, opp_dp, c], opp_recv)
    ring_steps(1, 0)
    for s in range(1, 5):
        for q in range(2):
            ring_steps(q, s)

    def relay(j):
        await_bytes(wg.at[j, 1 - hb, :, c], y_recv.at[j])
        block = wg.at[j, :, :, c]
        copy_to(block, block, s_send.at[j], s_recv.at[j], (dp, 1 - c, tm)).start()

    for load in loads:
        load.wait()
    for i in range(4):
        rows[i : i + 1] = vecs[i].reshape(1, D)
    rows[1:2] = 1.0 / jnp.sqrt(rows[1:2] + 1e-05)
    for p in pair:
        p.wait_recv()
    for side in range(2):
        await_bytes(xe.at[0:HALO], halo_recv.at[side])
        await_bytes(oe.at[0:GHALO], halo_recv.at[2 + side])
    t = lax.broadcasted_iota(jnp.int32, (WIDE, CW), 0) + (y * SPAN - HALO)
    keep = ((t >= 0) & (t < limit[0])).astype(F32)
    keep_mid = keep[HALO - GHALO : HALO + SPAN + GHALO]
    acc[...] = jnp.zeros_like(acc)

    def weights(j):
        return jnp.concatenate([wg[j, h].reshape(D, CW) for h in range(2)], axis=1)

    def channels(j):
        return pl.ds(pl.multiple_of(xl * HALF + j * CW, CW), CW)

    def forward(j):
        cs = channels(j)
        pre[j] = jnp.dot(xe[...], weights(j), preferred_element_type=F32)
        sg = lax.logistic(pre[j, :, CW:])
        gw[...] = (pre[j, :, :CW] * sg * keep).astype(BF16).astype(F32)
        pre[j, :, CW:] = sg
        mean, rstd, gain, bias = (rows[i : i + 1, cs] for i in range(4))
        scale = gain * rstd
        gs = jnp.zeros((8, CW), F32)
        bs = jnp.zeros((8, CW), F32)
        step = 96
        for r in range(0, MID, step):
            a = jnp.zeros((step, CW), F32)
            for k in range(KERNEL):
                a = a + ck[k : k + 1, cs] * gw[r + k + 1 : r + k + 1 + step, :]
            normed = (a - mean) * rstd
            act = normed * gain + bias
            sig = lax.logistic(act)
            ag = oe[r : r + step, pl.ds(pl.multiple_of(j * CW, CW), CW)].astype(F32)
            ag = ag * keep_mid[r : r + step] * sig * (1.0 + act * (1.0 - sig))
            cg[j, r : r + step] = (ag * scale).astype(BF16).astype(F32)
            lo, hi = max(r, GHALO) - r, min(r + step, GHALO + SPAN) - r
            gs = gs + jnp.sum((ag * normed)[lo:hi].reshape((hi - lo) // 8, 8, CW), axis=0)
            bs = bs + jnp.sum(ag[lo:hi].reshape((hi - lo) // 8, 8, CW), axis=0)
        sums = [jnp.zeros((8, CW), F32)] * KERNEL
        step = 64
        for r in range(0, SPAN, step):
            own = cg[j, GHALO + r : GHALO + r + step]
            for k in range(KERNEL):
                p = own * gw[r + k + 17 : r + k + 17 + step]
                sums[k] = sums[k] + jnp.sum(p.reshape(step // 8, 8, CW), axis=0)
        for k, total in enumerate(sums + [gs, bs]):
            parts[j, k : k + 1] = jnp.sum(total, axis=0, keepdims=True)
        parts[j, KERNEL + 2 :] = jnp.zeros((40 - KERNEL - 2, CW), F32)

        def give(i, carry):
            tile = 5 * j + i
            other, slot = lax.rem(tile, SUB), tile // SUB
            piece = parts.at[j, pl.ds(pl.multiple_of(8 * i, 8), 8)]

            @pl.when(other == mine)
            def _():
                rb1[slot, mine] = parts[j, pl.ds(pl.multiple_of(8 * i, 8), 8)]

            @pl.when(other != mine)
            def _():
                device = (dp, other % 2, (other // 2) * 2 + xl)
                copy_to(piece, rb1.at[slot, mine], r1_send, r1_recv.at[slot], device).start()

            return carry

        lax.fori_loop(0, 5, give, 0)

    def backward(j, first):
        cs = channels(j)
        near[...] = cg[j, pl.ds(pl.multiple_of(first, ROWS), ROWS + 2 * GHALO)]
        step = 64
        for r in range(0, ROWS, step):
            a = jnp.zeros((step, CW), F32)
            for k in range(KERNEL):
                a = a + ck[k : k + 1, cs] * near[r + 31 - k : r + 31 - k + step]
            t = lax.broadcasted_iota(jnp.int32, (step, CW), 0) + (y * SPAN + first + r)
            a = a * (t < limit[0]).astype(F32)
            at = pl.ds(pl.multiple_of(first + HALO + r, HALO), step)
            value, sg = pre[j, at, :CW], pre[j, at, CW:]
            a = a * sg
            pgr[r : r + step, :CW] = a.astype(BF16)
            pgr[r : r + step, CW:] = (a * value * (1.0 - sg)).astype(BF16)
        acc[pl.ds(pl.multiple_of(first, ROWS), ROWS)] += lax.dot_general(
            pgr[...], weights(j), (((1,), (1,)), ((), ())), preferred_element_type=F32
        )

    def backwards(lo, hi, first):
        def one(j, carry):
            backward(j, first)
            return carry

        lax.fori_loop(lo, hi, one, 0)

    def second(slot):
        await_bytes(rb1.at[slot, 0 : SUB - 1], r1_recv.at[slot])
        rb2[slot, dp] = jnp.sum(rb1[slot], axis=0)

        def spread(i, carry):
            piece = rb2.at[slot, dp]
            device = (lax.rem(dp + i, DP), c, tm)
            copy_to(piece, piece, r2_send.at[slot], r2_recv.at[slot], device).start()
            return carry

        lax.fori_loop(1, DP, spread, 0)

    def third(slot):
        await_bytes(rb2.at[slot, 0 : DP - 1], r2_recv.at[slot])
        index = xl * GROUP + slot * SUB + mine
        res[index] = jnp.sum(rb2[slot], axis=0) * (1.0 / 256.0)

        def share(i, carry):
            other = lax.rem(me + i, GROUP)
            piece = res.at[index]
            device = (dp, other % 2, other // 2)
            copy_to(piece, piece, r3_send.at[slot], r3_recv.at[slot], device).start()
            return carry

        lax.fori_loop(1, GROUP, share, 0)

    relay(0)
    relay(1)

    def chunk(j, carry):
        @pl.when(j + 2 < CHUNKS)
        def _():
            relay(j + 2)

        await_bytes(wg.at[j, :, :, 1 - c], s_recv.at[j])
        forward(j)
        return carry

    lax.fori_loop(0, CHUNKS, chunk, 0)

    there = pl.multiple_of((1 - xl) * ROWS, ROWS)
    second(0)
    backwards(0, CHUNKS // 2, there)

    @pl.when(mine < LAST)
    def _():
        second(1)

    backwards(CHUNKS // 2, CHUNKS, there)
    away[...] = acc[pl.ds(there, ROWS)].astype(BF16)
    give_back = copy_to(away, back, out_send, out_recv, partner)
    give_back.start()
    third(0)
    backwards(0, CHUNKS, own_at)

    @pl.when(mine < LAST)
    def _():
        third(1)

    give_back.wait()
    out[...] = (acc[here] + back[...].astype(F32)).astype(BF16)

    @pl.when(mine < LAST)
    def _():
        await_bytes(res.at[0 : 2 * LAST - 1], r3_recv.at[1])
        await_bytes(res.at[0 : TILES - 2], r1_send)
        await_bytes(rb2.at[1, 0 : DP - 1], r2_send.at[1])
        await_bytes(res.at[0 : GROUP - 1], r3_send.at[1])

    @pl.when(mine >= LAST)
    def _():
        await_bytes(res.at[0 : 2 * LAST], r3_recv.at[1])
        await_bytes(res.at[0 : TILES - 1], r1_send)

    await_bytes(res.at[0 : GROUP - 1], r3_recv.at[0])
    await_bytes(rb2.at[0, 0 : DP - 1], r2_send.at[0])
    await_bytes(res.at[0 : GROUP - 1], r3_send.at[0])
    for half in range(2):
        for j in range(CHUNKS):
            lo = half * HALF + j * CW
            cols = slice(lo, lo + CW)
            tile = half * GROUP + 5 * j
            for i in range(3):
                kernel_out[8 * i : 8 * i + 8, cols] = res[tile + i]
            kernel_out[24:KERNEL, cols] = res[tile + 3, 0:7]
            gain_out[:, cols] = res[tile + 3, 7:8]
            bias_out[:, cols] = res[tile + 4, 0:1]

    await_bytes(wg.at[:, hb, dp, c], opp_send)
    for p in pair:
        p.wait_send()
    for h in halos:
        h.wait_send()

    def sent(j, carry):
        await_bytes(wg.at[j, 0, 0:14, 0], z_send.at[j])
        await_bytes(wg.at[j, 0, :, 0], y_send.at[j])
        await_bytes(wg.at[j, :, :, c], s_send.at[j])
        return carry

    lax.fori_loop(0, CHUNKS, sent, 0)


def per_device(
    inputs, out_grad, proj_weight, conv_kernel, norm_mean, norm_var, norm_gain, norm_bias, lengths
):
    vmem = pl.BlockSpec(memory_space=pltpu.VMEM)
    dma = pltpu.SemaphoreType.DMA
    whole = pl.BlockSpec(memory_space=pltpu.HBM)
    grad, kernel_grad, gain_grad, bias_grad = pl.pallas_call(
        kernel,
        out_shape=(
            jax.ShapeDtypeStruct((ROWS, D), BF16),
            jax.ShapeDtypeStruct((KERNEL, D), F32),
            jax.ShapeDtypeStruct((1, D), F32),
            jax.ShapeDtypeStruct((1, D), F32),
        ),
        in_specs=[pl.BlockSpec(memory_space=pltpu.SMEM)] + [whole] * 8,
        out_specs=(vmem,) * 4,
        scratch_shapes=[
            pltpu.VMEM((CHUNKS, 2, DP, CHAN, SHARD, CW), BF16),
            pltpu.VMEM((WIDE, D), BF16),
            pltpu.VMEM((MID, HALF), BF16),
            pltpu.VMEM((KERNEL, D), F32),
            pltpu.VMEM((4, D), F32),
            pltpu.VMEM((8, D), F32),
            pltpu.VMEM((CHUNKS, WIDE, 2 * CW), F32),
            pltpu.VMEM((WIDE, CW), F32),
            pltpu.VMEM((CHUNKS, MID, CW), F32),
            pltpu.VMEM((ROWS + 2 * GHALO, CW), F32),
            pltpu.VMEM((ROWS, 2 * CW), BF16),
            pltpu.VMEM((SPAN, D), F32),
            pltpu.VMEM((ROWS, D), BF16),
            pltpu.VMEM((ROWS, D), BF16),
            pltpu.VMEM((CHUNKS, 40, CW), F32),
            pltpu.VMEM((2, SUB, 8, CW), F32),
            pltpu.VMEM((2, DP, 8, CW), F32),
            pltpu.VMEM((2 * GROUP, 8, CW), F32),
            dma((7,)), dma((CHUNKS,)),
            dma((2,)), dma((2,)),
            dma((4,)), dma((4,)),
            dma, dma,
            dma((CHUNKS,)), dma((2, 2, CHUNKS, 4)),
            dma((CHUNKS,)), dma((CHUNKS,)),
            dma((CHUNKS,)), dma((CHUNKS,)),
            dma, dma((2,)),
            dma((2,)), dma((2,)),
            dma((2,)), dma((2,)),
            dma, dma,
        ],
        compiler_params=pltpu.CompilerParams(
            collective_id=0, has_side_effects=True, vmem_limit_bytes=60 << 20
        ),
    )(
        lengths, inputs.reshape(ROWS, D), out_grad.reshape(ROWS, D), proj_weight, conv_kernel,
        norm_mean, norm_var, norm_gain, norm_bias,
    )
    return (
        grad.reshape(1, 1, ROWS, D),
        kernel_grad,
        gain_grad.reshape(D),
        bias_grad.reshape(D),
    )


def solution(mesh):
    in_specs = (
        P("dp", "chan", "tm", None),
        P("dp", "chan", "tm", None),
        P(("dp", "chan"), None),
        P(),
        P(),
        P(),
        P(),
        P(),
        P("dp"),
    )
    out_specs = (P("dp", "chan", "tm", None), P(), P(), P())
    return jax.shard_map(
        per_device, mesh=mesh, in_specs=in_specs, out_specs=out_specs, check_vma=False
    )
```

```python
import functools

import jax
import jax.numpy as jnp
from jax import lax
from jax.experimental import pallas as pl
from jax.experimental.pallas import tpu as pltpu
from jax.sharding import PartitionSpec as P

MESH = pl.DeviceIdType.MESH
D = 1536
KERNEL = 31
FRAMES = 2048
ROWS = 128
SPAN = 2 * ROWS
HALO = 32
GHALO = 16
WIDE = SPAN + 2 * HALO
MID = SPAN + 2 * GHALO
SHARD = 48
CW = 128
HALF = D // 2
CHUNKS = HALF // CW
DP, CHAN, TM = 16, 2, 16
GROUP = TM * CHAN
SUB = GROUP // 2
F32 = jnp.float32
BF16 = jnp.bfloat16
TILES = CHUNKS * 5
SET = CHUNKS // 2
LAST = TILES - SUB


def copy_to(src, dst, send, recv, device):
    return pltpu.make_async_remote_copy(
        src_ref=src, dst_ref=dst, send_sem=send, recv_sem=recv, device_id=device, device_id_type=MESH
    )


def await_bytes(ref, sem):
    pltpu.make_async_copy(ref, ref, sem).wait()


def kernel(
    limit, x_in, og_in, w_in, ck_in, mean_in, var_in, gain_in, bias_in,
    out, sums_out,
    wg, xe, oe, ck, vecs, rows, pre, gw, cg, near, pgr, acc, away, back, parts, rb1, rb2, res,
    in_sem, w_sem, pair_send, pair_recv, halo_send, halo_recv, opp_send, opp_recv, z_send, z_recv,
    y_send, y_recv, s_send, s_recv, r1_send, r1_recv, r2_send, r2_recv, r3_send, r3_recv,
    out_send, out_recv,
):
    dp, c, tm = lax.axis_index("dp"), lax.axis_index("chan"), lax.axis_index("tm")
    z, xh, y, xl = dp // 2, dp % 2, tm // 2, tm % 2
    opp_dp = dp + 1 - 2 * xh
    hc = xl + xh - 2 * xl * xh
    opposite = (opp_dp, c, tm + 1 - 2 * xl)
    partner = (dp, c, tm + 1 - 2 * xl)
    me = tm * CHAN + c
    mine = y * CHAN + c
    hb = y % 2

    def weight_cols(half, j):
        return pl.ds(pl.multiple_of(hb * D + half * HALF + j * CW, CW), CW)

    def own_rows(j):
        return pltpu.make_async_copy(
            w_in.at[:, weight_cols(hc, j)], wg.at[j, hb, dp, c], w_sem.at[j]
        )

    def fetch(j, carry):
        own_rows(j).start()
        return carry

    lax.fori_loop(0, CHUNKS, fetch, 0)
    own_at = pl.multiple_of(xl * ROWS, ROWS)
    here = pl.ds(own_at, ROWS)
    x_rows = xe.at[pl.ds(pl.multiple_of(HALO + xl * ROWS, HALO), ROWS)]
    og_rows = oe.at[pl.ds(pl.multiple_of(GHALO + xl * ROWS, GHALO), ROWS)]

    def half_cols(half):
        return pl.ds(pl.multiple_of(half * HALF, HALF), HALF)

    loads = [
        pltpu.make_async_copy(src, dst, in_sem.at[i])
        for i, (src, dst) in enumerate(
            (
                (x_in, x_rows),
                (og_in.at[:, half_cols(hc)], og_rows),
                (ck_in, ck),
                (mean_in, vecs.at[0]),
                (var_in, vecs.at[1]),
                (gain_in, vecs.at[2]),
                (bias_in, vecs.at[3]),
            )
        )
    ]
    for load in loads:
        load.start()

    def same_channels(i):
        other = lax.rem(dp + i, DP)
        return (other, c, 2 * y + hc + other % 2 - 2 * hc * (other % 2))

    barrier = pltpu.get_barrier_semaphore()

    def greet(i, carry):
        other = lax.rem(me + i, GROUP)
        pl.semaphore_signal(
            barrier, inc=1, device_id=(dp, other % 2, other // 2), device_id_type=MESH
        )
        return carry

    def greet_dp(i, carry):
        pl.semaphore_signal(barrier, inc=1, device_id=same_channels(i), device_id_type=MESH)
        return carry

    lax.fori_loop(1, DP, greet_dp, 0)
    lax.fori_loop(1, GROUP, greet, 0)
    pl.semaphore_wait(barrier, GROUP + DP - 2)

    def fetched(j, carry):
        own_rows(j).wait()
        return carry

    lax.fori_loop(0, CHUNKS, fetched, 0)

    up = (lax.rem(dp + 2, DP), c, tm)
    down = (lax.rem(dp + DP - 2, DP), c, tm)
    y_even = y + 1 - 2 * (y % 2)
    y_odd = lax.rem(y + 7 + 2 * (y % 2), 8)

    sibling = (dp, 1 - c, tm)
    sharers = [(dp, c, other * 2 + xl) for other in (y_even, y_odd)]

    def weight_block(g, dz, part):
        return wg.at[g * SET : (g + 1) * SET, hb, 2 * lax.rem(z + dz, 8) + part, c]

    def pass_on(block, g, d, q, s):
        recv = y_recv.at[g, d, q, s]
        copy_to(block, block, y_send.at[g], recv, sharers[g]).start()
        copy_to(block, block, s_send.at[g], s_recv.at[g], sibling).start()

    def ring_step(g, s):
        for d, (steps, sign, device) in enumerate(((4 - g, 7, up), (3 + g, 1, down))):
            block = weight_block(g, sign * s, xh)
            if 0 < s <= steps:
                await_bytes(block, z_recv.at[d, g, s - 1])
            if s < steps:
                copy_to(block, block, z_send.at[g], z_recv.at[d, g, s], device).start()
            if s <= steps and s + 1 > d:
                copy_to(block, block, opp_send.at[g], opp_recv.at[d, g, s], opposite).start()
                pass_on(block, g, d, 0, s)

    def opp_step(g, s):
        for d, (steps, sign) in enumerate(((4 - g, 7), (3 + g, 1))):
            if s <= steps and s + 1 > d:
                block = weight_block(g, sign * s, 1 - xh)
                await_bytes(block, opp_recv.at[d, g, s])
                pass_on(block, g, d, 1, s)

    def y_step(g, q, s):
        for d, (steps, sign) in enumerate(((4 - g, 7), (3 + g, 1))):
            if s <= steps and s + 1 > d:
                dz = 2 * lax.rem(z + sign * s, 8) + (xh + q - 2 * q * xh)
                block = wg.at[g * SET : (g + 1) * SET, 1 - hb, dz, c]
                await_bytes(block, y_recv.at[g, d, q, s])
                copy_to(block, block, s_send.at[g], s_recv.at[g], sibling).start()

    def each(step, s):
        for g in range(2):
            step(g, s)

    each(ring_step, 0)

    pair = (
        copy_to(x_in, x_rows, pair_send.at[0], pair_recv.at[0], partner),
        copy_to(
            og_in.at[:, half_cols(1 - hc)], og_rows, pair_send.at[1], pair_recv.at[1], partner
        ),
    )
    for p in pair:
        p.start()
    beyond = lax.rem(y + 7 + 2 * xl, 8) * 2
    x_edge = x_in.at[pl.ds(pl.multiple_of(xl * (ROWS - HALO), HALO), HALO)]
    x_far = xe.at[pl.ds(pl.multiple_of((1 - xl) * (HALO + SPAN), HALO), HALO)]
    og_edge = pl.ds(pl.multiple_of(xl * (ROWS - GHALO), GHALO), GHALO)
    og_far = oe.at[pl.ds(pl.multiple_of((1 - xl) * (GHALO + SPAN), GHALO), GHALO)]
    halos = []
    for other in range(2):
        device = (dp, c, beyond + other)
        halos.append(copy_to(x_edge, x_far, halo_send.at[other], halo_recv.at[xl], device))
        halos.append(
            copy_to(
                og_in.at[og_edge, half_cols(xh if other == 0 else 1 - xh)], og_far,
                halo_send.at[2 + other], halo_recv.at[2 + xl], device,
            )
        )
    for h in halos:
        h.start()

    each(ring_step, 1)
    for s in range(2, 5):
        each(opp_step, s - 2)
        each(ring_step, s)
        for q in range(2):
            if s - 2 - q >= 0:
                each(lambda g, t, q=q: y_step(g, q, t), s - 2 - q)
    each(opp_step, 3)
    each(lambda g, t: y_step(g, 0, t), 3)
    each(opp_step, 4)

    def last_steps(g):
        y_step(g, 1, 2)
        y_step(g, 0, 4)
        y_step(g, 1, 3)
        y_step(g, 1, 4)

    def await_sibling(g):
        await_bytes(wg.at[g * SET : (g + 1) * SET, :, :, 1 - c], s_recv.at[g])

    for load in loads:
        load.wait()
    for i in range(4):
        rows[i : i + 1] = vecs[i].reshape(1, D)
    rows[1:2] = 1.0 / jnp.sqrt(rows[1:2] + 1e-05)
    for p in pair:
        p.wait_recv()
    for side in range(2):
        await_bytes(xe.at[0:HALO], halo_recv.at[side])
        await_bytes(oe.at[0:GHALO], halo_recv.at[2 + side])
    t = lax.broadcasted_iota(jnp.int32, (WIDE, CW), 0) + (y * SPAN - HALO)
    keep = ((t >= 0) & (t < limit[0])).astype(F32)
    keep_mid = keep[HALO - GHALO : HALO + SPAN + GHALO]
    acc[...] = jnp.zeros_like(acc)

    def weights(j):
        return jnp.concatenate([wg[j, h].reshape(D, CW) for h in range(2)], axis=1)

    def channels(j):
        return pl.ds(pl.multiple_of(hc * HALF + j * CW, CW), CW)

    def forward(j):
        cs = channels(j)
        pre[j] = jnp.dot(xe[...], weights(j), preferred_element_type=F32)
        sg = lax.logistic(pre[j, :, CW:])
        gw[...] = (pre[j, :, :CW] * sg * keep).astype(BF16).astype(F32)
        pre[j, :, CW:] = sg
        mean, rstd, gain, bias = (rows[i : i + 1, cs] for i in range(4))
        scale = gain * rstd
        gs = jnp.zeros((8, CW), F32)
        bs = jnp.zeros((8, CW), F32)
        step = 96
        for r in range(0, MID, step):
            a = jnp.zeros((step, CW), F32)
            for k in range(KERNEL):
                a = a + ck[k : k + 1, cs] * gw[r + k + 1 : r + k + 1 + step, :]
            normed = (a - mean) * rstd
            act = normed * gain + bias
            sig = lax.logistic(act)
            ag = oe[r : r + step, pl.ds(pl.multiple_of(j * CW, CW), CW)].astype(F32)
            ag = ag * keep_mid[r : r + step] * sig * (1.0 + act * (1.0 - sig))
            cg[j, r : r + step] = (ag * scale).astype(BF16).astype(F32)
            lo, hi = max(r, GHALO) - r, min(r + step, GHALO + SPAN) - r
            gs = gs + jnp.sum((ag * normed)[lo:hi].reshape((hi - lo) // 8, 8, CW), axis=0)
            bs = bs + jnp.sum(ag[lo:hi].reshape((hi - lo) // 8, 8, CW), axis=0)
        sums = [jnp.zeros((8, CW), F32)] * KERNEL
        step = 64
        for r in range(0, SPAN, step):
            own = cg[j, GHALO + r : GHALO + r + step]
            for k in range(KERNEL):
                p = own * gw[r + k + 17 : r + k + 17 + step]
                sums[k] = sums[k] + jnp.sum(p.reshape(step // 8, 8, CW), axis=0)
        for k, total in enumerate(sums + [gs, bs]):
            parts[j, k : k + 1] = jnp.sum(total, axis=0, keepdims=True)
        parts[j, KERNEL + 2 :] = jnp.zeros((40 - KERNEL - 2, CW), F32)

        def give(i, carry):
            tile = 5 * j + i
            other, slot = lax.rem(tile, SUB), tile // SUB
            piece = parts.at[j, pl.ds(pl.multiple_of(8 * i, 8), 8)]

            @pl.when(other == mine)
            def _():
                rb1[slot, mine] = parts[j, pl.ds(pl.multiple_of(8 * i, 8), 8)]

            @pl.when(other != mine)
            def _():
                device = (dp, other % 2, (other // 2) * 2 + xl)
                copy_to(piece, rb1.at[slot, mine], r1_send, r1_recv.at[slot], device).start()

            return carry

        lax.fori_loop(0, 5, give, 0)

    def backward(j, first):
        cs = channels(j)
        near[...] = cg[j, pl.ds(pl.multiple_of(first, ROWS), ROWS + 2 * GHALO)]
        step = 64
        for r in range(0, ROWS, step):
            a = jnp.zeros((step, CW), F32)
            for k in range(KERNEL):
                a = a + ck[k : k + 1, cs] * near[r + 31 - k : r + 31 - k + step]
            t = lax.broadcasted_iota(jnp.int32, (step, CW), 0) + (y * SPAN + first + r)
            a = a * (t < limit[0]).astype(F32)
            at = pl.ds(pl.multiple_of(first + HALO + r, HALO), step)
            value, sg = pre[j, at, :CW], pre[j, at, CW:]
            a = a * sg
            pgr[r : r + step, :CW] = a.astype(BF16)
            pgr[r : r + step, CW:] = (a * value * (1.0 - sg)).astype(BF16)
        acc[pl.ds(pl.multiple_of(first, ROWS), ROWS)] += lax.dot_general(
            pgr[...], weights(j), (((1,), (1,)), ((), ())), preferred_element_type=F32
        )

    def backwards(lo, hi, first):
        def one(j, carry):
            backward(j, first)
            return carry

        lax.fori_loop(lo, hi, one, 0)

    def second(slot):
        await_bytes(rb1.at[slot, 0 : SUB - 1], r1_recv.at[slot])
        rb2[slot, dp] = jnp.sum(rb1[slot], axis=0)

        def spread(i, carry):
            i = DP // 2 + (2 * (i % 2) - 1) * (i // 2)
            piece = rb2.at[slot, dp]
            device = same_channels(i)
            copy_to(piece, piece, r2_send.at[slot], r2_recv.at[slot], device).start()
            return carry

        lax.fori_loop(1, DP, spread, 0)

    def third(slot):
        await_bytes(rb2.at[slot, 0 : DP - 1], r2_recv.at[slot])
        index = hc * GROUP + slot * SUB + mine
        res[index] = jnp.sum(rb2[slot], axis=0) * (1.0 / 256.0)

        def share(i, carry):
            other = lax.rem(me + SUB + (2 * (i % 2) - 1) * (i // 2), GROUP)
            piece = res.at[index]
            device = (dp, other % 2, other // 2)
            copy_to(piece, piece, r3_send.at[slot], r3_recv.at[slot], device).start()
            return carry

        lax.fori_loop(1, GROUP, share, 0)

    last_steps(0)
    last_steps(1)
    await_sibling(0)

    def chunk(j, carry):
        @pl.when(j == SET)
        def _():
            await_sibling(1)

        forward(j)
        return carry

    lax.fori_loop(0, CHUNKS, chunk, 0)

    there = pl.multiple_of((1 - xl) * ROWS, ROWS)
    second(0)
    backwards(0, CHUNKS // 2, there)

    @pl.when(mine < LAST)
    def _():
        second(1)

    backwards(CHUNKS // 2, CHUNKS, there)
    away[...] = acc[pl.ds(there, ROWS)].astype(BF16)
    give_back = copy_to(away, back, out_send, out_recv, partner)
    give_back.start()
    third(0)
    backwards(0, CHUNKS, own_at)

    @pl.when(mine < LAST)
    def _():
        third(1)

    give_back.wait()
    out[...] = (acc[here] + back[...].astype(F32)).astype(BF16)

    @pl.when(mine < LAST)
    def _():
        await_bytes(res.at[0 : 2 * LAST - 1], r3_recv.at[1])
        await_bytes(res.at[0 : TILES - 2], r1_send)
        await_bytes(rb2.at[1, 0 : DP - 1], r2_send.at[1])
        await_bytes(res.at[0 : GROUP - 1], r3_send.at[1])

    @pl.when(mine >= LAST)
    def _():
        await_bytes(res.at[0 : 2 * LAST], r3_recv.at[1])
        await_bytes(res.at[0 : TILES - 1], r1_send)

    await_bytes(res.at[0 : GROUP - 1], r3_recv.at[0])
    await_bytes(rb2.at[0, 0 : DP - 1], r2_send.at[0])
    await_bytes(res.at[0 : GROUP - 1], r3_send.at[0])
    sums_out[...] = res[...]

    for p in pair:
        p.wait_send()
    for h in halos:
        h.wait_send()

    for g in range(2):
        await_bytes(wg.at[0:SET, 0, 0:7, 0], z_send.at[g])
        await_bytes(wg.at[0:SET, 0, 0:8, 0], opp_send.at[g])
        await_bytes(wg.at[0:SET, 0, :, 0], y_send.at[g])
        await_bytes(wg.at[0:SET, :, :, 0], s_send.at[g])


def finish(grad, sums, out, kernel_out, gain_out, bias_out):
    out[...] = grad[...]
    for half in range(2):
        for j in range(CHUNKS):
            lo = half * HALF + j * CW
            cols = slice(lo, lo + CW)
            tile = half * GROUP + 5 * j
            for i in range(3):
                kernel_out[8 * i : 8 * i + 8, cols] = sums[tile + i]
            kernel_out[24:KERNEL, cols] = sums[tile + 3, 0:7]
            gain_out[cols] = sums[tile + 3, 7]
            bias_out[cols] = sums[tile + 4, 0]


def per_device(
    inputs, out_grad, proj_weight, conv_kernel, norm_mean, norm_var, norm_gain, norm_bias, lengths
):
    vmem = pl.BlockSpec(memory_space=pltpu.VMEM)
    dma = pltpu.SemaphoreType.DMA
    whole = pl.BlockSpec(memory_space=pltpu.HBM)
    grad, sums = pl.pallas_call(
        kernel,
        out_shape=(
            jax.ShapeDtypeStruct((ROWS, D), BF16),
            jax.ShapeDtypeStruct((2 * GROUP, 8, CW), F32),
        ),
        in_specs=[pl.BlockSpec(memory_space=pltpu.SMEM)] + [whole] * 8,
        out_specs=(vmem,) * 2,
        scratch_shapes=[
            pltpu.VMEM((CHUNKS, 2, DP, CHAN, SHARD, CW), BF16),
            pltpu.VMEM((WIDE, D), BF16),
            pltpu.VMEM((MID, HALF), BF16),
            pltpu.VMEM((KERNEL, D), F32),
            pltpu.VMEM((4, D), F32),
            pltpu.VMEM((8, D), F32),
            pltpu.VMEM((CHUNKS, WIDE, 2 * CW), F32),
            pltpu.VMEM((WIDE, CW), F32),
            pltpu.VMEM((CHUNKS, MID, CW), F32),
            pltpu.VMEM((ROWS + 2 * GHALO, CW), F32),
            pltpu.VMEM((ROWS, 2 * CW), BF16),
            pltpu.VMEM((SPAN, D), F32),
            pltpu.VMEM((ROWS, D), BF16),
            pltpu.VMEM((ROWS, D), BF16),
            pltpu.VMEM((CHUNKS, 40, CW), F32),
            pltpu.VMEM((2, SUB, 8, CW), F32),
            pltpu.VMEM((2, DP, 8, CW), F32),
            pltpu.VMEM((2 * GROUP, 8, CW), F32),
            dma((7,)), dma((CHUNKS,)),
            dma((2,)), dma((2,)),
            dma((4,)), dma((4,)),
            dma((2,)), dma((2, 2, 5)),
            dma((2,)), dma((2, 2, 4)),
            dma((2,)), dma((2, 2, 2, 5)),
            dma((2,)), dma((2,)),
            dma, dma((2,)),
            dma((2,)), dma((2,)),
            dma((2,)), dma((2,)),
            dma, dma,
        ],
        compiler_params=pltpu.CompilerParams(
            collective_id=0, has_side_effects=True, vmem_limit_bytes=60 << 20
        ),
    )(
        lengths, inputs.reshape(ROWS, D), out_grad.reshape(ROWS, D), proj_weight, conv_kernel,
        norm_mean, norm_var, norm_gain, norm_bias,
    )
    grad, kernel_grad, gain_grad, bias_grad = pl.pallas_call(
        finish,
        out_shape=(
            jax.ShapeDtypeStruct((ROWS, D), BF16),
            jax.ShapeDtypeStruct((KERNEL, D), F32),
            jax.ShapeDtypeStruct((D,), F32),
            jax.ShapeDtypeStruct((D,), F32),
        ),
    )(grad, sums)
    return grad.reshape(1, 1, ROWS, D), kernel_grad, gain_grad, bias_grad


def solution(mesh):
    in_specs = (
        P("dp", "chan", "tm", None),
        P("dp", "chan", "tm", None),
        P(("dp", "chan"), None),
        P(),
        P(),
        P(),
        P(),
        P(),
        P("dp"),
    )
    out_specs = (P("dp", "chan", "tm", None), P(), P(), P())
    return jax.shard_map(
        per_device, mesh=mesh, in_specs=in_specs, out_specs=out_specs, check_vma=False
    )
```

```python
import functools

import jax
import jax.numpy as jnp
from jax import lax
from jax.experimental import pallas as pl
from jax.experimental.pallas import tpu as pltpu
from jax.sharding import PartitionSpec as P

MESH = pl.DeviceIdType.MESH
D = 1536
KERNEL = 31
FRAMES = 2048
ROWS = 128
SPAN = 2 * ROWS
HALO = 32
GHALO = 16
WIDE = SPAN + 2 * HALO
MID = SPAN + 2 * GHALO
SHARD = 48
CW = 128
HALF = D // 2
CHUNKS = HALF // CW
DP, CHAN, TM = 16, 2, 16
GROUP = TM * CHAN
SUB = GROUP // 2
F32 = jnp.float32
BF16 = jnp.bfloat16
TILES = CHUNKS * 5
PAIRS = CHUNKS // 2
SET = CHUNKS // 2
LAST = TILES - SUB


def copy_to(src, dst, send, recv, device):
    return pltpu.make_async_remote_copy(
        src_ref=src, dst_ref=dst, send_sem=send, recv_sem=recv, device_id=device, device_id_type=MESH
    )


def await_bytes(ref, sem):
    pltpu.make_async_copy(ref, ref, sem).wait()


def kernel(
    limit, x_in, og_in, w_in, ck_in, mean_in, var_in, gain_in, bias_in,
    out, sums_out,
    wg, xe, oe, ck, vecs, rows, pre_even, pre_odd, gw, cg, near, pgr, acc, away, back, parts, rb1, rb2, res,
    in_sem, w_sem, pair_send, pair_recv, halo_send, halo_recv, opp_send, opp_recv, z_send, z_recv,
    y_send, y_recv, s_send, s_recv, r1_send, r1_recv, r2_send, r2_recv, r3_send, r3_recv,
    out_send, out_recv,
):
    dp, c, tm = lax.axis_index("dp"), lax.axis_index("chan"), lax.axis_index("tm")
    z, xh, y, xl = dp // 2, dp % 2, tm // 2, tm % 2
    opp_dp = dp + 1 - 2 * xh
    hc = xl + xh - 2 * xl * xh
    opposite = (opp_dp, c, tm + 1 - 2 * xl)
    partner = (dp, c, tm + 1 - 2 * xl)
    me = tm * CHAN + c
    mine = y * CHAN + c
    hb = y % 2

    def weight_cols(half, j):
        return pl.ds(pl.multiple_of(hb * D + half * HALF + j * CW, CW), CW)

    def own_rows(j):
        return pltpu.make_async_copy(
            w_in.at[:, weight_cols(hc, j)], wg.at[j, hb, dp, c], w_sem.at[j]
        )

    def fetch(j, carry):
        own_rows(j).start()
        return carry

    lax.fori_loop(0, CHUNKS, fetch, 0)
    own_at = pl.multiple_of(xl * ROWS, ROWS)
    here = pl.ds(own_at, ROWS)
    x_rows = xe.at[pl.ds(pl.multiple_of(HALO + xl * ROWS, HALO), ROWS)]
    og_rows = oe.at[pl.ds(pl.multiple_of(GHALO + xl * ROWS, GHALO), ROWS)]

    def half_cols(half):
        return pl.ds(pl.multiple_of(half * HALF, HALF), HALF)

    loads = [
        pltpu.make_async_copy(src, dst, in_sem.at[i])
        for i, (src, dst) in enumerate(
            (
                (x_in, x_rows),
                (og_in.at[:, half_cols(hc)], og_rows),
                (ck_in, ck),
                (mean_in, vecs.at[0]),
                (var_in, vecs.at[1]),
                (gain_in, vecs.at[2]),
                (bias_in, vecs.at[3]),
            )
        )
    ]
    for load in loads:
        load.start()

    def same_channels(i):
        other = lax.rem(dp + i, DP)
        return (other, c, 2 * y + hc + other % 2 - 2 * hc * (other % 2))

    barrier = pltpu.get_barrier_semaphore()

    def greet(i, carry):
        other = lax.rem(me + i, GROUP)
        pl.semaphore_signal(
            barrier, inc=1, device_id=(dp, other % 2, other // 2), device_id_type=MESH
        )
        return carry

    def greet_dp(i, carry):
        pl.semaphore_signal(barrier, inc=1, device_id=same_channels(i), device_id_type=MESH)
        return carry

    lax.fori_loop(1, DP, greet_dp, 0)
    lax.fori_loop(1, GROUP, greet, 0)
    pl.semaphore_wait(barrier, GROUP + DP - 2)

    def fetched(j, carry):
        own_rows(j).wait()
        return carry

    lax.fori_loop(0, CHUNKS, fetched, 0)

    up = (lax.rem(dp + 2, DP), c, tm)
    down = (lax.rem(dp + DP - 2, DP), c, tm)
    y_even = y + 1 - 2 * (y % 2)
    y_odd = lax.rem(y + 7 + 2 * (y % 2), 8)

    sibling = (dp, 1 - c, tm)
    sharers = [(dp, c, other * 2 + xl) for other in (y_even, y_odd)]

    def weight_block(g, dz, part):
        return wg.at[g * SET : (g + 1) * SET, hb, 2 * lax.rem(z + dz, 8) + part, c]

    def pass_on(block, g, d, q, s):
        recv = y_recv.at[g, d, q, s]
        copy_to(block, block, y_send.at[g], recv, sharers[g]).start()
        copy_to(block, block, s_send.at[g], s_recv.at[g], sibling).start()

    def ring_step(g, s):
        for d, (steps, sign, device) in enumerate(((4 - g, 7, up), (3 + g, 1, down))):
            block = weight_block(g, sign * s, xh)
            if 0 < s <= steps:
                await_bytes(block, z_recv.at[d, g, s - 1])
            if s < steps:
                copy_to(block, block, z_send.at[g], z_recv.at[d, g, s], device).start()
            if s <= steps and s + 1 > d:
                copy_to(block, block, opp_send.at[g], opp_recv.at[d, g, s], opposite).start()
                pass_on(block, g, d, 0, s)

    def opp_step(g, s):
        for d, (steps, sign) in enumerate(((4 - g, 7), (3 + g, 1))):
            if s <= steps and s + 1 > d:
                block = weight_block(g, sign * s, 1 - xh)
                await_bytes(block, opp_recv.at[d, g, s])
                pass_on(block, g, d, 1, s)

    def y_step(g, q, s):
        for d, (steps, sign) in enumerate(((4 - g, 7), (3 + g, 1))):
            if s <= steps and s + 1 > d:
                dz = 2 * lax.rem(z + sign * s, 8) + (xh + q - 2 * q * xh)
                block = wg.at[g * SET : (g + 1) * SET, 1 - hb, dz, c]
                await_bytes(block, y_recv.at[g, d, q, s])
                copy_to(block, block, s_send.at[g], s_recv.at[g], sibling).start()

    def each(step, s):
        for g in range(2):
            step(g, s)

    each(ring_step, 0)

    pair = (
        copy_to(x_in, x_rows, pair_send.at[0], pair_recv.at[0], partner),
        copy_to(
            og_in.at[:, half_cols(1 - hc)], og_rows, pair_send.at[1], pair_recv.at[1], partner
        ),
    )
    for p in pair:
        p.start()
    beyond = lax.rem(y + 7 + 2 * xl, 8) * 2
    x_edge = x_in.at[pl.ds(pl.multiple_of(xl * (ROWS - HALO), HALO), HALO)]
    x_far = xe.at[pl.ds(pl.multiple_of((1 - xl) * (HALO + SPAN), HALO), HALO)]
    og_edge = pl.ds(pl.multiple_of(xl * (ROWS - GHALO), GHALO), GHALO)
    og_far = oe.at[pl.ds(pl.multiple_of((1 - xl) * (GHALO + SPAN), GHALO), GHALO)]
    halos = []
    for other in range(2):
        device = (dp, c, beyond + other)
        halos.append(copy_to(x_edge, x_far, halo_send.at[other], halo_recv.at[xl], device))
        halos.append(
            copy_to(
                og_in.at[og_edge, half_cols(xh if other == 0 else 1 - xh)], og_far,
                halo_send.at[2 + other], halo_recv.at[2 + xl], device,
            )
        )
    for h in halos:
        h.start()

    each(ring_step, 1)
    for s in range(2, 5):
        each(opp_step, s - 2)
        each(ring_step, s)
        for q in range(2):
            if s - 2 - q >= 0:
                each(lambda g, t, q=q: y_step(g, q, t), s - 2 - q)
    each(opp_step, 3)
    each(lambda g, t: y_step(g, 0, t), 3)
    each(opp_step, 4)

    def last_steps(g):
        y_step(g, 1, 2)
        y_step(g, 0, 4)
        y_step(g, 1, 3)
        y_step(g, 1, 4)

    def await_sibling(g):
        await_bytes(wg.at[g * SET : (g + 1) * SET, :, :, 1 - c], s_recv.at[g])

    for load in loads:
        load.wait()
    for i in range(4):
        rows[i : i + 1] = vecs[i].reshape(1, D)
    rows[1:2] = 1.0 / jnp.sqrt(rows[1:2] + 1e-05)
    for p in pair:
        p.wait_recv()
    for side in range(2):
        await_bytes(xe.at[0:HALO], halo_recv.at[side])
        await_bytes(oe.at[0:GHALO], halo_recv.at[2 + side])
    t = lax.broadcasted_iota(jnp.int32, (WIDE, CW), 0) + (y * SPAN - HALO)
    keep = ((t >= 0) & (t < limit[0])).astype(F32)
    keep_mid = keep[HALO - GHALO : HALO + SPAN + GHALO]
    acc[...] = jnp.zeros_like(acc)

    def weights(j):
        return jnp.concatenate([wg[j, h].reshape(D, CW) for h in range(2)], axis=1)

    def channels(j):
        return pl.ds(pl.multiple_of(hc * HALF + j * CW, CW), CW)

    def project(pre, i, j):
        pre[i] = jnp.dot(xe[...], weights(j), preferred_element_type=F32)

    def forward(pre, i, j):
        cs = channels(j)
        sg = lax.logistic(pre[i, :, CW:])
        gw[...] = (pre[i, :, :CW] * sg * keep).astype(BF16).astype(F32)
        pre[i, :, CW:] = sg
        mean, rstd, gain, bias = (rows[i : i + 1, cs] for i in range(4))
        scale = gain * rstd
        gs = jnp.zeros((8, CW), F32)
        bs = jnp.zeros((8, CW), F32)
        step = 96
        for r in range(0, MID, step):
            a = jnp.zeros((step, CW), F32)
            for k in range(KERNEL):
                a = a + ck[k : k + 1, cs] * gw[r + k + 1 : r + k + 1 + step, :]
            normed = (a - mean) * rstd
            act = normed * gain + bias
            sig = lax.logistic(act)
            ag = oe[r : r + step, pl.ds(pl.multiple_of(j * CW, CW), CW)].astype(F32)
            ag = ag * keep_mid[r : r + step] * sig * (1.0 + act * (1.0 - sig))
            cg[j, r : r + step] = (ag * scale).astype(BF16).astype(F32)
            lo, hi = max(r, GHALO) - r, min(r + step, GHALO + SPAN) - r
            gs = gs + jnp.sum((ag * normed)[lo:hi].reshape((hi - lo) // 8, 8, CW), axis=0)
            bs = bs + jnp.sum(ag[lo:hi].reshape((hi - lo) // 8, 8, CW), axis=0)
        sums = [jnp.zeros((8, CW), F32)] * KERNEL
        step = 64
        for r in range(0, SPAN, step):
            own = cg[j, GHALO + r : GHALO + r + step]
            for k in range(KERNEL):
                p = own * gw[r + k + 17 : r + k + 17 + step]
                sums[k] = sums[k] + jnp.sum(p.reshape(step // 8, 8, CW), axis=0)
        for k, total in enumerate(sums + [gs, bs]):
            parts[j, k : k + 1] = jnp.sum(total, axis=0, keepdims=True)
        parts[j, KERNEL + 2 :] = jnp.zeros((40 - KERNEL - 2, CW), F32)

        def give(i, carry):
            tile = 5 * j + i
            other, slot = lax.rem(tile, SUB), tile // SUB
            piece = parts.at[j, pl.ds(pl.multiple_of(8 * i, 8), 8)]

            @pl.when(other == mine)
            def _():
                rb1[slot, mine] = parts[j, pl.ds(pl.multiple_of(8 * i, 8), 8)]

            @pl.when(other != mine)
            def _():
                device = (dp, other % 2, (other // 2) * 2 + xl)
                copy_to(piece, rb1.at[slot, mine], r1_send, r1_recv.at[slot], device).start()

            return carry

        lax.fori_loop(0, 5, give, 0)

    def backward(pre, i, j, first):
        cs = channels(j)
        near[...] = cg[j, pl.ds(pl.multiple_of(first, ROWS), ROWS + 2 * GHALO)]
        step = 64
        for r in range(0, ROWS, step):
            a = jnp.zeros((step, CW), F32)
            for k in range(KERNEL):
                a = a + ck[k : k + 1, cs] * near[r + 31 - k : r + 31 - k + step]
            t = lax.broadcasted_iota(jnp.int32, (step, CW), 0) + (y * SPAN + first + r)
            a = a * (t < limit[0]).astype(F32)
            at = pl.ds(pl.multiple_of(first + HALO + r, HALO), step)
            value, sg = pre[i, at, :CW], pre[i, at, CW:]
            a = a * sg
            pgr[r : r + step, :CW] = a.astype(BF16)
            pgr[r : r + step, CW:] = (a * value * (1.0 - sg)).astype(BF16)
        acc[pl.ds(pl.multiple_of(first, ROWS), ROWS)] += lax.dot_general(
            pgr[...], weights(j), (((1,), (1,)), ((), ())), preferred_element_type=F32
        )

    def backwards(lo, hi, first):
        def one(i, carry):
            backward(pre_even, i, 2 * i, first)
            backward(pre_odd, i, 2 * i + 1, first)
            return carry

        lax.fori_loop(lo, hi, one, 0)

    def second(slot):
        await_bytes(rb1.at[slot, 0 : SUB - 1], r1_recv.at[slot])
        rb2[slot, dp] = jnp.sum(rb1[slot], axis=0)

        def spread(i, carry):
            i = DP // 2 + (2 * (i % 2) - 1) * (i // 2)
            piece = rb2.at[slot, dp]
            device = same_channels(i)
            copy_to(piece, piece, r2_send.at[slot], r2_recv.at[slot], device).start()
            return carry

        lax.fori_loop(1, DP, spread, 0)

    def third(slot):
        await_bytes(rb2.at[slot, 0 : DP - 1], r2_recv.at[slot])
        index = hc * GROUP + slot * SUB + mine
        res[index] = jnp.sum(rb2[slot], axis=0) * (1.0 / 256.0)

        def share(i, carry):
            other = lax.rem(me + SUB + (2 * (i % 2) - 1) * (i // 2), GROUP)
            piece = res.at[index]
            device = (dp, other % 2, other // 2)
            copy_to(piece, piece, r3_send.at[slot], r3_recv.at[slot], device).start()
            return carry

        lax.fori_loop(1, GROUP, share, 0)

    last_steps(0)
    last_steps(1)
    await_sibling(0)

    def chunks(i, carry):
        @pl.when(i == SET // 2)
        def _():
            await_sibling(1)

        project(pre_odd, i, 2 * i + 1)
        forward(pre_even, i, 2 * i)
        project(pre_even, i + 1, jnp.minimum(2 * i + 2, CHUNKS - 1))
        forward(pre_odd, i, 2 * i + 1)
        return carry

    project(pre_even, 0, 0)
    lax.fori_loop(0, PAIRS, chunks, 0)

    there = pl.multiple_of((1 - xl) * ROWS, ROWS)
    second(0)
    backwards(0, 1, there)

    @pl.when(mine < LAST)
    def _():
        second(1)

    backwards(1, PAIRS, there)
    away[...] = acc[pl.ds(there, ROWS)].astype(BF16)
    give_back = copy_to(away, back, out_send, out_recv, partner)
    give_back.start()
    third(0)
    backwards(0, 1, own_at)

    @pl.when(mine < LAST)
    def _():
        third(1)

    backwards(1, PAIRS, own_at)

    give_back.wait()
    out[...] = (acc[here] + back[...].astype(F32)).astype(BF16)

    @pl.when(mine < LAST)
    def _():
        await_bytes(res.at[0 : 2 * LAST - 1], r3_recv.at[1])
        await_bytes(res.at[0 : TILES - 2], r1_send)
        await_bytes(rb2.at[1, 0 : DP - 1], r2_send.at[1])
        await_bytes(res.at[0 : GROUP - 1], r3_send.at[1])

    @pl.when(mine >= LAST)
    def _():
        await_bytes(res.at[0 : 2 * LAST], r3_recv.at[1])
        await_bytes(res.at[0 : TILES - 1], r1_send)

    await_bytes(res.at[0 : GROUP - 1], r3_recv.at[0])
    await_bytes(rb2.at[0, 0 : DP - 1], r2_send.at[0])
    await_bytes(res.at[0 : GROUP - 1], r3_send.at[0])
    sums_out[...] = res[...]

    for p in pair:
        p.wait_send()
    for h in halos:
        h.wait_send()

    for g in range(2):
        await_bytes(wg.at[0:SET, 0, 0:7, 0], z_send.at[g])
        await_bytes(wg.at[0:SET, 0, 0:8, 0], opp_send.at[g])
        await_bytes(wg.at[0:SET, 0, :, 0], y_send.at[g])
        await_bytes(wg.at[0:SET, :, :, 0], s_send.at[g])


def finish(grad, sums, out, kernel_out, gain_out, bias_out):
    out[...] = grad[...]
    for half in range(2):
        for j in range(CHUNKS):
            lo = half * HALF + j * CW
            cols = slice(lo, lo + CW)
            tile = half * GROUP + 5 * j
            for i in range(3):
                kernel_out[8 * i : 8 * i + 8, cols] = sums[tile + i]
            kernel_out[24:KERNEL, cols] = sums[tile + 3, 0:7]
            gain_out[cols] = sums[tile + 3, 7]
            bias_out[cols] = sums[tile + 4, 0]


def per_device(
    inputs, out_grad, proj_weight, conv_kernel, norm_mean, norm_var, norm_gain, norm_bias, lengths
):
    vmem = pl.BlockSpec(memory_space=pltpu.VMEM)
    dma = pltpu.SemaphoreType.DMA
    whole = pl.BlockSpec(memory_space=pltpu.HBM)
    grad, sums = pl.pallas_call(
        kernel,
        out_shape=(
            jax.ShapeDtypeStruct((ROWS, D), BF16),
            jax.ShapeDtypeStruct((2 * GROUP, 8, CW), F32),
        ),
        in_specs=[pl.BlockSpec(memory_space=pltpu.SMEM)] + [whole] * 8,
        out_specs=(vmem,) * 2,
        scratch_shapes=[
            pltpu.VMEM((CHUNKS, 2, DP, CHAN, SHARD, CW), BF16),
            pltpu.VMEM((WIDE, D), BF16),
            pltpu.VMEM((MID, HALF), BF16),
            pltpu.VMEM((KERNEL, D), F32),
            pltpu.VMEM((4, D), F32),
            pltpu.VMEM((8, D), F32),
            pltpu.VMEM((PAIRS + 1, WIDE, 2 * CW), F32),
            pltpu.VMEM((PAIRS, WIDE, 2 * CW), F32),
            pltpu.VMEM((WIDE, CW), F32),
            pltpu.VMEM((CHUNKS, MID, CW), F32),
            pltpu.VMEM((ROWS + 2 * GHALO, CW), F32),
            pltpu.VMEM((ROWS, 2 * CW), BF16),
            pltpu.VMEM((SPAN, D), F32),
            pltpu.VMEM((ROWS, D), BF16),
            pltpu.VMEM((ROWS, D), BF16),
            pltpu.VMEM((CHUNKS, 40, CW), F32),
            pltpu.VMEM((2, SUB, 8, CW), F32),
            pltpu.VMEM((2, DP, 8, CW), F32),
            pltpu.VMEM((2 * GROUP, 8, CW), F32),
            dma((7,)), dma((CHUNKS,)),
            dma((2,)), dma((2,)),
            dma((4,)), dma((4,)),
            dma((2,)), dma((2, 2, 5)),
            dma((2,)), dma((2, 2, 4)),
            dma((2,)), dma((2, 2, 2, 5)),
            dma((2,)), dma((2,)),
            dma, dma((2,)),
            dma((2,)), dma((2,)),
            dma((2,)), dma((2,)),
            dma, dma,
        ],
        compiler_params=pltpu.CompilerParams(
            collective_id=0, has_side_effects=True, vmem_limit_bytes=60 << 20
        ),
    )(
        lengths, inputs.reshape(ROWS, D), out_grad.reshape(ROWS, D), proj_weight, conv_kernel,
        norm_mean, norm_var, norm_gain, norm_bias,
    )
    grad, kernel_grad, gain_grad, bias_grad = pl.pallas_call(
        finish,
        out_shape=(
            jax.ShapeDtypeStruct((ROWS, D), BF16),
            jax.ShapeDtypeStruct((KERNEL, D), F32),
            jax.ShapeDtypeStruct((D,), F32),
            jax.ShapeDtypeStruct((D,), F32),
        ),
    )(grad, sums)
    return grad.reshape(1, 1, ROWS, D), kernel_grad, gain_grad, bias_grad


def solution(mesh):
    in_specs = (
        P("dp", "chan", "tm", None),
        P("dp", "chan", "tm", None),
        P(("dp", "chan"), None),
        P(),
        P(),
        P(),
        P(),
        P(),
        P("dp"),
    )
    out_specs = (P("dp", "chan", "tm", None), P(), P(), P())
    return jax.shard_map(
        per_device, mesh=mesh, in_specs=in_specs, out_specs=out_specs, check_vma=False
    )
```

```python
import functools

import jax
import jax.numpy as jnp
from jax import lax
from jax.experimental import pallas as pl
from jax.experimental.pallas import tpu as pltpu
from jax.sharding import PartitionSpec as P

MESH = pl.DeviceIdType.MESH
D = 1536
KERNEL = 31
FRAMES = 2048
ROWS = 128
SPAN = 2 * ROWS
HALO = 32
GHALO = 16
WIDE = SPAN + 2 * HALO
MID = SPAN + 2 * GHALO
SHARD = 48
CW = 128
HALF = D // 2
CHUNKS = HALF // CW
DP, CHAN, TM = 16, 2, 16
GROUP = TM * CHAN
SUB = GROUP // 2
F32 = jnp.float32
BF16 = jnp.bfloat16
TILES = CHUNKS * 5
PAIRS = CHUNKS // 2
SET = CHUNKS // 2
LAST = TILES - SUB


def copy_to(src, dst, send, recv, device):
    return pltpu.make_async_remote_copy(
        src_ref=src, dst_ref=dst, send_sem=send, recv_sem=recv, device_id=device, device_id_type=MESH
    )


def await_bytes(ref, sem):
    pltpu.make_async_copy(ref, ref, sem).wait()


def kernel(
    limit, x_in, og_in, w_in, ck_in, mean_in, var_in, gain_in, bias_in,
    out, sums_out,
    wg, xe, oe, ck, vecs, rows, pre_even, pre_odd, gw, cg, near, pgr, acc, away, back, parts, rb1, rb2, res,
    in_sem, w_sem, pair_send, pair_recv, halo_send, halo_recv, opp_send, opp_recv, z_send, z_recv,
    y_send, y_recv, s_send, s_recv, r1_send, r1_recv, r2_send, r2_recv, r3_send, r3_recv,
    out_send, out_recv,
):
    dp, c, tm = lax.axis_index("dp"), lax.axis_index("chan"), lax.axis_index("tm")
    z, xh, y, xl = dp // 2, dp % 2, tm // 2, tm % 2
    opp_dp = dp + 1 - 2 * xh
    hc = xl + xh - 2 * xl * xh
    opposite = (opp_dp, c, tm + 1 - 2 * xl)
    partner = (dp, c, tm + 1 - 2 * xl)
    me = tm * CHAN + c
    mine = y * CHAN + c
    hb = y % 2

    def weight_cols(half, j):
        return pl.ds(pl.multiple_of(hb * D + half * HALF + j * CW, CW), CW)

    def own_rows(j):
        return pltpu.make_async_copy(
            w_in.at[:, weight_cols(hc, j)], wg.at[j, hb, dp, c], w_sem.at[j]
        )

    def fetch(j, carry):
        own_rows(j).start()
        return carry

    lax.fori_loop(0, CHUNKS, fetch, 0)
    own_at = pl.multiple_of(xl * ROWS, ROWS)
    here = pl.ds(own_at, ROWS)
    x_rows = xe.at[pl.ds(pl.multiple_of(HALO + xl * ROWS, HALO), ROWS)]
    og_rows = oe.at[pl.ds(pl.multiple_of(GHALO + xl * ROWS, GHALO), ROWS)]

    def half_cols(half):
        return pl.ds(pl.multiple_of(half * HALF, HALF), HALF)

    loads = [
        pltpu.make_async_copy(src, dst, in_sem.at[i])
        for i, (src, dst) in enumerate(
            (
                (x_in, x_rows),
                (og_in.at[:, half_cols(hc)], og_rows),
                (ck_in, ck),
                (mean_in, vecs.at[0]),
                (var_in, vecs.at[1]),
                (gain_in, vecs.at[2]),
                (bias_in, vecs.at[3]),
            )
        )
    ]
    for load in loads:
        load.start()

    def same_channels(i):
        other = lax.rem(dp + i, DP)
        return (other, c, 2 * y + hc + other % 2 - 2 * hc * (other % 2))

    barrier = pltpu.get_barrier_semaphore()

    def greet(i, carry):
        other = lax.rem(me + i, GROUP)
        pl.semaphore_signal(
            barrier, inc=1, device_id=(dp, other % 2, other // 2), device_id_type=MESH
        )
        return carry

    def greet_dp(i, carry):
        pl.semaphore_signal(barrier, inc=1, device_id=same_channels(i), device_id_type=MESH)
        return carry

    lax.fori_loop(1, DP, greet_dp, 0)
    lax.fori_loop(1, GROUP, greet, 0)
    pl.semaphore_wait(barrier, GROUP + DP - 2)

    def fetched(j, carry):
        own_rows(j).wait()
        return carry

    lax.fori_loop(0, CHUNKS, fetched, 0)

    up = (lax.rem(dp + 2, DP), c, tm)
    down = (lax.rem(dp + DP - 2, DP), c, tm)
    y_even = y + 1 - 2 * (y % 2)
    y_odd = lax.rem(y + 7 + 2 * (y % 2), 8)

    sibling = (dp, 1 - c, tm)
    sharers = [(dp, c, other * 2 + xl) for other in (y_even, y_odd)]

    def weight_block(g, dz, part):
        return wg.at[g * SET : (g + 1) * SET, hb, 2 * lax.rem(z + dz, 8) + part, c]

    def pass_on(block, g, d, q, s):
        recv = y_recv.at[g, d, q, s]
        copy_to(block, block, y_send.at[g], recv, sharers[g]).start()
        copy_to(block, block, s_send.at[g], s_recv.at[g], sibling).start()

    def ring_step(g, s):
        for d, (steps, sign, device) in enumerate(((4 - g, 7, up), (3 + g, 1, down))):
            block = weight_block(g, sign * s, xh)
            if 0 < s <= steps:
                await_bytes(block, z_recv.at[d, g, s - 1])
            if s < steps:
                copy_to(block, block, z_send.at[g], z_recv.at[d, g, s], device).start()
            if s <= steps and s + 1 > d:
                copy_to(block, block, opp_send.at[g], opp_recv.at[d, g, s], opposite).start()
                pass_on(block, g, d, 0, s)

    def opp_step(g, s):
        for d, (steps, sign) in enumerate(((4 - g, 7), (3 + g, 1))):
            if s <= steps and s + 1 > d:
                block = weight_block(g, sign * s, 1 - xh)
                await_bytes(block, opp_recv.at[d, g, s])
                pass_on(block, g, d, 1, s)

    def y_step(g, q, s):
        for d, (steps, sign) in enumerate(((4 - g, 7), (3 + g, 1))):
            if s <= steps and s + 1 > d:
                dz = 2 * lax.rem(z + sign * s, 8) + (xh + q - 2 * q * xh)
                block = wg.at[g * SET : (g + 1) * SET, 1 - hb, dz, c]
                await_bytes(block, y_recv.at[g, d, q, s])
                copy_to(block, block, s_send.at[g], s_recv.at[g], sibling).start()

    def each(step, s):
        for g in range(2):
            step(g, s)

    each(ring_step, 0)

    pair = (
        copy_to(x_in, x_rows, pair_send.at[0], pair_recv.at[0], partner),
        copy_to(
            og_in.at[:, half_cols(1 - hc)], og_rows, pair_send.at[1], pair_recv.at[1], partner
        ),
    )
    for p in pair:
        p.start()
    beyond = lax.rem(y + 7 + 2 * xl, 8) * 2
    x_edge = x_in.at[pl.ds(pl.multiple_of(xl * (ROWS - HALO), HALO), HALO)]
    x_far = xe.at[pl.ds(pl.multiple_of((1 - xl) * (HALO + SPAN), HALO), HALO)]
    og_edge = pl.ds(pl.multiple_of(xl * (ROWS - GHALO), GHALO), GHALO)
    og_far = oe.at[pl.ds(pl.multiple_of((1 - xl) * (GHALO + SPAN), GHALO), GHALO)]
    halos = []
    for other in range(2):
        device = (dp, c, beyond + other)
        halos.append(copy_to(x_edge, x_far, halo_send.at[other], halo_recv.at[xl], device))
        halos.append(
            copy_to(
                og_in.at[og_edge, half_cols(xh if other == 0 else 1 - xh)], og_far,
                halo_send.at[2 + other], halo_recv.at[2 + xl], device,
            )
        )
    for h in halos:
        h.start()

    each(ring_step, 1)
    for s in range(2, 5):
        each(opp_step, s - 2)
        each(ring_step, s)
        for q in range(2):
            if s - 2 - q >= 0:
                each(lambda g, t, q=q: y_step(g, q, t), s - 2 - q)
    each(opp_step, 3)
    each(lambda g, t: y_step(g, 0, t), 3)
    each(opp_step, 4)

    def last_steps(g):
        y_step(g, 1, 2)
        y_step(g, 0, 4)
        y_step(g, 1, 3)
        y_step(g, 1, 4)

    def await_sibling(g):
        await_bytes(wg.at[g * SET : (g + 1) * SET, :, :, 1 - c], s_recv.at[g])

    for load in loads:
        load.wait()
    for i in range(4):
        rows[i : i + 1] = vecs[i].reshape(1, D)
    rows[1:2] = 1.0 / jnp.sqrt(rows[1:2] + 1e-05)
    for p in pair:
        p.wait_recv()
    for side in range(2):
        await_bytes(xe.at[0:HALO], halo_recv.at[side])
        await_bytes(oe.at[0:GHALO], halo_recv.at[2 + side])
    t = lax.broadcasted_iota(jnp.int32, (WIDE, CW), 0) + (y * SPAN - HALO)
    keep = ((t >= 0) & (t < limit[0])).astype(F32)
    keep_mid = keep[HALO - GHALO : HALO + SPAN + GHALO]
    acc[...] = jnp.zeros_like(acc)

    def weights(j):
        return jnp.concatenate([wg[j, h].reshape(D, CW) for h in range(2)], axis=1)

    def channels(j):
        return pl.ds(pl.multiple_of(hc * HALF + j * CW, CW), CW)

    def project(pre, i, j):
        pre[i] = jnp.dot(xe[...], weights(j), preferred_element_type=F32)

    def forward(pre, i, j):
        cs = channels(j)
        sg = lax.logistic(pre[i, :, CW:])
        gw[...] = (pre[i, :, :CW] * sg * keep).astype(BF16).astype(F32)
        pre[i, :, CW:] = sg
        mean, rstd, gain, bias = (rows[i : i + 1, cs] for i in range(4))
        scale = gain * rstd
        gs = jnp.zeros((8, CW), F32)
        bs = jnp.zeros((8, CW), F32)
        step = 96
        for r in range(0, MID, step):
            a = jnp.zeros((step, CW), F32)
            for k in range(KERNEL):
                a = a + ck[k : k + 1, cs] * gw[r + k + 1 : r + k + 1 + step, :]
            normed = (a - mean) * rstd
            act = normed * gain + bias
            sig = lax.logistic(act)
            ag = oe[r : r + step, pl.ds(pl.multiple_of(j * CW, CW), CW)].astype(F32)
            ag = ag * keep_mid[r : r + step] * sig * (1.0 + act * (1.0 - sig))
            cg[j, r : r + step] = (ag * scale).astype(BF16).astype(F32)
            lo, hi = max(r, GHALO) - r, min(r + step, GHALO + SPAN) - r
            gs = gs + jnp.sum((ag * normed)[lo:hi].reshape((hi - lo) // 8, 8, CW), axis=0)
            bs = bs + jnp.sum(ag[lo:hi].reshape((hi - lo) // 8, 8, CW), axis=0)
        sums = [jnp.zeros((8, CW), F32)] * KERNEL
        step = 64
        for r in range(0, SPAN, step):
            own = cg[j, GHALO + r : GHALO + r + step]
            for k in range(KERNEL):
                p = own * gw[r + k + 17 : r + k + 17 + step]
                sums[k] = sums[k] + jnp.sum(p.reshape(step // 8, 8, CW), axis=0)
        for k, total in enumerate(sums + [gs, bs]):
            parts[j, k : k + 1] = jnp.sum(total, axis=0, keepdims=True)
        parts[j, KERNEL + 2 :] = jnp.zeros((40 - KERNEL - 2, CW), F32)

        def give(i, carry):
            tile = 5 * j + i
            other, slot = lax.rem(tile, SUB), tile // SUB
            piece = parts.at[j, pl.ds(pl.multiple_of(8 * i, 8), 8)]

            @pl.when(other == mine)
            def _():
                rb1[slot, mine] = parts[j, pl.ds(pl.multiple_of(8 * i, 8), 8)]

            @pl.when(other != mine)
            def _():
                device = (dp, other % 2, (other // 2) * 2 + xl)
                copy_to(piece, rb1.at[slot, mine], r1_send, r1_recv.at[slot], device).start()

            return carry

        lax.fori_loop(0, 5, give, 0)

    def backward(pre, i, j, first):
        cs = channels(j)
        near[...] = cg[j, pl.ds(pl.multiple_of(first, ROWS), ROWS + 2 * GHALO)]
        step = 64
        for r in range(0, ROWS, step):
            a = jnp.zeros((step, CW), F32)
            for k in range(KERNEL):
                a = a + ck[k : k + 1, cs] * near[r + 31 - k : r + 31 - k + step]
            t = lax.broadcasted_iota(jnp.int32, (step, CW), 0) + (y * SPAN + first + r)
            a = a * (t < limit[0]).astype(F32)
            at = pl.ds(pl.multiple_of(first + HALO + r, HALO), step)
            value, sg = pre[i, at, :CW], pre[i, at, CW:]
            a = a * sg
            pgr[r : r + step, :CW] = a.astype(BF16)
            pgr[r : r + step, CW:] = (a * value * (1.0 - sg)).astype(BF16)
        acc[pl.ds(pl.multiple_of(first, ROWS), ROWS)] += lax.dot_general(
            pgr[...], weights(j), (((1,), (1,)), ((), ())), preferred_element_type=F32
        )

    def backwards(lo, hi, first):
        def one(i, carry):
            backward(pre_even, i, 2 * i, first)
            backward(pre_odd, i, 2 * i + 1, first)
            return carry

        lax.fori_loop(lo, hi, one, 0)

    def second(slot):
        await_bytes(rb1.at[slot, 0 : SUB - 1], r1_recv.at[slot])
        rb2[slot, dp] = jnp.sum(rb1[slot], axis=0)

        def spread(i, carry):
            i = DP // 2 + (2 * (i % 2) - 1) * (i // 2)
            piece = rb2.at[slot, dp]
            device = same_channels(i)
            copy_to(piece, piece, r2_send.at[slot], r2_recv.at[slot], device).start()
            return carry

        lax.fori_loop(1, DP, spread, 0)

    def third(slot):
        await_bytes(rb2.at[slot, 0 : DP - 1], r2_recv.at[slot])
        index = hc * GROUP + slot * SUB + mine
        res[index] = jnp.sum(rb2[slot], axis=0) * (1.0 / 256.0)

        def share(i, carry):
            other = lax.rem(me + SUB + (2 * (i % 2) - 1) * (i // 2), GROUP)
            piece = res.at[index]
            device = (dp, other % 2, other // 2)
            copy_to(piece, piece, r3_send.at[slot], r3_recv.at[slot], device).start()
            return carry

        lax.fori_loop(1, GROUP, share, 0)

    last_steps(0)
    await_sibling(0)

    def chunks(i, carry):
        @pl.when(i == SET // 2)
        def _():
            await_sibling(1)

        project(pre_odd, i, 2 * i + 1)
        forward(pre_even, i, 2 * i)
        project(pre_even, i + 1, jnp.minimum(2 * i + 2, CHUNKS - 1))
        forward(pre_odd, i, 2 * i + 1)
        return carry

    project(pre_even, 0, 0)
    last_steps(1)
    lax.fori_loop(0, PAIRS, chunks, 0)

    there = pl.multiple_of((1 - xl) * ROWS, ROWS)
    second(0)
    backwards(0, 1, there)

    @pl.when(mine < LAST)
    def _():
        second(1)

    backwards(1, PAIRS, there)
    away[...] = acc[pl.ds(there, ROWS)].astype(BF16)
    give_back = copy_to(away, back, out_send, out_recv, partner)
    give_back.start()
    third(0)
    backwards(0, 1, own_at)

    @pl.when(mine < LAST)
    def _():
        third(1)

    backwards(1, PAIRS, own_at)

    give_back.wait()
    out[...] = (acc[here] + back[...].astype(F32)).astype(BF16)

    @pl.when(mine < LAST)
    def _():
        await_bytes(res.at[0 : 2 * LAST - 1], r3_recv.at[1])
        await_bytes(res.at[0 : TILES - 2], r1_send)
        await_bytes(rb2.at[1, 0 : DP - 1], r2_send.at[1])
        await_bytes(res.at[0 : GROUP - 1], r3_send.at[1])

    @pl.when(mine >= LAST)
    def _():
        await_bytes(res.at[0 : 2 * LAST], r3_recv.at[1])
        await_bytes(res.at[0 : TILES - 1], r1_send)

    await_bytes(res.at[0 : GROUP - 1], r3_recv.at[0])
    await_bytes(rb2.at[0, 0 : DP - 1], r2_send.at[0])
    await_bytes(res.at[0 : GROUP - 1], r3_send.at[0])
    sums_out[...] = res[...]

    for p in pair:
        p.wait_send()
    for h in halos:
        h.wait_send()

    for g in range(2):
        await_bytes(wg.at[0:SET, 0, 0:7, 0], z_send.at[g])
        await_bytes(wg.at[0:SET, 0, 0:8, 0], opp_send.at[g])
        await_bytes(wg.at[0:SET, 0, :, 0], y_send.at[g])
        await_bytes(wg.at[0:SET, :, :, 0], s_send.at[g])


def finish(grad, sums, out, kernel_out, gain_out, bias_out):
    out[...] = grad[...]
    for half in range(2):
        for j in range(CHUNKS):
            lo = half * HALF + j * CW
            cols = slice(lo, lo + CW)
            tile = half * GROUP + 5 * j
            for i in range(3):
                kernel_out[8 * i : 8 * i + 8, cols] = sums[tile + i]
            kernel_out[24:KERNEL, cols] = sums[tile + 3, 0:7]
            gain_out[cols] = sums[tile + 3, 7]
            bias_out[cols] = sums[tile + 4, 0]


def per_device(
    inputs, out_grad, proj_weight, conv_kernel, norm_mean, norm_var, norm_gain, norm_bias, lengths
):
    vmem = pl.BlockSpec(memory_space=pltpu.VMEM)
    dma = pltpu.SemaphoreType.DMA
    whole = pl.BlockSpec(memory_space=pltpu.HBM)
    grad, sums = pl.pallas_call(
        kernel,
        out_shape=(
            jax.ShapeDtypeStruct((ROWS, D), BF16),
            jax.ShapeDtypeStruct((2 * GROUP, 8, CW), F32),
        ),
        in_specs=[pl.BlockSpec(memory_space=pltpu.SMEM)] + [whole] * 8,
        out_specs=(vmem,) * 2,
        scratch_shapes=[
            pltpu.VMEM((CHUNKS, 2, DP, CHAN, SHARD, CW), BF16),
            pltpu.VMEM((WIDE, D), BF16),
            pltpu.VMEM((MID, HALF), BF16),
            pltpu.VMEM((KERNEL, D), F32),
            pltpu.VMEM((4, D), F32),
            pltpu.VMEM((8, D), F32),
            pltpu.VMEM((PAIRS + 1, WIDE, 2 * CW), F32),
            pltpu.VMEM((PAIRS, WIDE, 2 * CW), F32),
            pltpu.VMEM((WIDE, CW), F32),
            pltpu.VMEM((CHUNKS, MID, CW), F32),
            pltpu.VMEM((ROWS + 2 * GHALO, CW), F32),
            pltpu.VMEM((ROWS, 2 * CW), BF16),
            pltpu.VMEM((SPAN, D), F32),
            pltpu.VMEM((ROWS, D), BF16),
            pltpu.VMEM((ROWS, D), BF16),
            pltpu.VMEM((CHUNKS, 40, CW), F32),
            pltpu.VMEM((2, SUB, 8, CW), F32),
            pltpu.VMEM((2, DP, 8, CW), F32),
            pltpu.VMEM((2 * GROUP, 8, CW), F32),
            dma((7,)), dma((CHUNKS,)),
            dma((2,)), dma((2,)),
            dma((4,)), dma((4,)),
            dma((2,)), dma((2, 2, 5)),
            dma((2,)), dma((2, 2, 4)),
            dma((2,)), dma((2, 2, 2, 5)),
            dma((2,)), dma((2,)),
            dma, dma((2,)),
            dma((2,)), dma((2,)),
            dma((2,)), dma((2,)),
            dma, dma,
        ],
        compiler_params=pltpu.CompilerParams(
            collective_id=0, has_side_effects=True, vmem_limit_bytes=60 << 20
        ),
    )(
        lengths, inputs.reshape(ROWS, D), out_grad.reshape(ROWS, D), proj_weight, conv_kernel,
        norm_mean, norm_var, norm_gain, norm_bias,
    )
    grad, kernel_grad, gain_grad, bias_grad = pl.pallas_call(
        finish,
        out_shape=(
            jax.ShapeDtypeStruct((ROWS, D), BF16),
            jax.ShapeDtypeStruct((KERNEL, D), F32),
            jax.ShapeDtypeStruct((D,), F32),
            jax.ShapeDtypeStruct((D,), F32),
        ),
    )(grad, sums)
    return grad.reshape(1, 1, ROWS, D), kernel_grad, gain_grad, bias_grad


def solution(mesh):
    in_specs = (
        P("dp", "chan", "tm", None),
        P("dp", "chan", "tm", None),
        P(("dp", "chan"), None),
        P(),
        P(),
        P(),
        P(),
        P(),
        P("dp"),
    )
    out_specs = (P("dp", "chan", "tm", None), P(), P(), P())
    return jax.shard_map(
        per_device, mesh=mesh, in_specs=in_specs, out_specs=out_specs, check_vma=False
    )
```
